32 devices in a mesh: segment: 4 (over z), ctx: 4 (over x, core), tp: 2 (over y).
Axes of the slice: x: 2, y: 2, z: 4, core: 2. Of those that a mesh axis runs over, the one named last changes fastest.
Arguments:
- hidden_in: bfloat16 [4, 512, 4096], P('segment', 'ctx')
- norm_gain: bfloat16 [4, 4096], P('segment'), may hold values from 0.5 to 1.5
- query_weight: bfloat16 [4, 4096, 4096], P('segment', None, 'tp')
- keyval_weight: bfloat16 [4, 4096, 2048], P('segment', None, 'tp')
- output_weight: bfloat16 [4, 4096, 4096], P('segment', 'tp'), may hold values from -0.1875 to 0.1875
- windows: int32 [4], P('segment'), may hold values from 192 to 384, as said below
Outputs:
- handed: bfloat16 [4, 512, 4096], P('segment', 'ctx', 'tp')
The draws below stay inside these ranges and needn't reach their ends.
Inputs may be any that keep to these rules, and one draw needn't show every extreme that they name: `windows`: one section's window is exactly 384 tokens.
All inputs are finite; a program needn't handle non-finite values.
Results may differ from the reference program's by a relative error of at most 0.006.
The reference program's roundings to bfloat16 on the way count: a program that leaves them out, or rounds other values in their place, can miss the bound.
Values may be sent and summed in bfloat16 or wider, within the bound.
No kernel may reach another device: no remote copies, remote signals or barrier semaphores. Data moves between devices by JAX's collectives and lax.ppermute only.
A program may use at most 128 MiB of HBM per device.

```python
import math
import jax
import jax.numpy as jnp
from jax import lax

D = 4096
HD = 128
QHEADS = 32
KVHEADS = 8
TOKENS = 512
WINMAX = 384
N_SEGMENT = 4


def feature_count():
    return min(64, D // 4)


def plant_scale():
    return math.sqrt(2000.0 / (0.9 * D * feature_count() * math.sqrt(HD)))


def draw_hidden_in(key, part):
    base_key, sink_key, strength_key, factor_key = jax.random.split(key, 4)
    shape = (N_SEGMENT, TOKENS, D)
    sinks = jax.random.uniform(sink_key, (N_SEGMENT, TOKENS, 1), jnp.float32) < 0.125
    base = jnp.clip(jax.random.normal(base_key, shape, jnp.float32), -6.0, 6.0)
    strength = jax.random.uniform(strength_key, (N_SEGMENT, TOKENS, 1), jnp.float32, 1.5, 3.0)
    factor = jax.random.uniform(factor_key, shape, jnp.float32, 0.8, 1.2)
    leading = (jnp.arange(D) < feature_count())[None, None, :]
    massive = strength * math.sqrt(D / feature_count()) * factor
    return jnp.where(sinks & leading, massive, base).astype(jnp.bfloat16)


def planted_weight(key, shape, chosen_columns):
    base_key, plant_key = jax.random.split(key)
    spread = D ** (-0.5)
    base = jnp.clip(jax.random.normal(base_key, shape, jnp.float32), -6.0, 6.0) * spread
    planted = plant_scale() * jax.random.uniform(plant_key, shape, jnp.float32, 0.8, 1.2)
    leading = (jnp.arange(D) < feature_count())[None, :, None]
    return jnp.where(leading & chosen_columns[None, None, :], planted, base).astype(jnp.bfloat16)


def draw_query_weight(key, part):
    column = jnp.arange(QHEADS * HD) % HD
    chosen = column % (HD // 2) >= HD // 2 - HD // 8
    return planted_weight(key, (N_SEGMENT, D, QHEADS * HD), chosen)


def draw_keyval_weight(key, part):
    column = jnp.arange(KVHEADS * 2 * HD) % (2 * HD)
    chosen = (column < HD) & (column % (HD // 2) >= HD // 2 - HD // 8)
    return planted_weight(key, (N_SEGMENT, D, KVHEADS * 2 * HD), chosen)


def draw_windows(key, part):
    first_key, second_key = jax.random.split(key)
    lengths = jax.random.randint(first_key, (N_SEGMENT,), WINMAX // 2, WINMAX + 1)
    chosen = jax.random.randint(second_key, (), 0, N_SEGMENT)
    return jnp.where(jnp.arange(N_SEGMENT) == chosen, WINMAX, lengths).astype(jnp.int32)


def steps_of(key, shape, cuts, smallest, top_value):
    loudness, own = 1.0, jax.random.fold_in(key, 6)
    for axis_at, blocks in cuts:
        heights = jnp.exp(jax.random.uniform(jax.random.fold_in(own, axis_at), (blocks,), jnp.float32, smallest / len(cuts), top_value / len(cuts)))
        loudness = loudness * jnp.repeat(heights, shape[axis_at] // blocks).reshape([-1 if axis == axis_at else 1 for axis in range(len(shape))])
    return loudness


def noise(own_key, dims, deviation, bound, cuts=(), kind=jnp.bfloat16):
    values = jax.random.normal(own_key, dims, jnp.float32) * deviation
    if len(cuts) > 0:
        values = steps_of(own_key, dims, cuts, -0.22, 0.18) * values
    return jnp.clip(values, min=-bound, max=bound).astype(kind)


def setup_inputs(seed: int = 0) -> dict:
    seeds = jax.random.split(jax.random.key(seed), 7)
    hidden_in = draw_hidden_in(jax.random.fold_in(seeds[6], 71), 0)
    norm_gain = jnp.clip(1.0 + 0.1 * jax.random.normal(seeds[1], (N_SEGMENT, D), jnp.float32), 0.5, 1.5).astype(jnp.bfloat16)
    query_weight = draw_query_weight(jax.random.fold_in(seeds[6], 71), 0)
    keyval_weight = draw_keyval_weight(jax.random.fold_in(seeds[6], 71), 0)
    output_weight = noise(seeds[4], (N_SEGMENT, QHEADS * HD, D), (QHEADS * HD // 4) ** -0.5, 0.1875, ((0, 4), (1, 2)))
    windows = draw_windows(jax.random.fold_in(seeds[6], 71), 0)
    return {"hidden_in": hidden_in, "norm_gain": norm_gain, "query_weight": query_weight, "keyval_weight": keyval_weight, "output_weight": output_weight, "windows": windows}


NORM_EPS = 1e-05

def rotate(vector, positions):
    half_dim = vector.shape[-1] // 2
    inverse = 10000.0 ** (-jnp.arange(half_dim, dtype=jnp.float32) / half_dim)
    angles = positions.astype(jnp.float32)[:, None, None] * inverse[None, None, :]
    cosine = jnp.cos(angles)
    sine = jnp.sin(angles)
    first_half = vector[..., :half_dim]
    second_half = vector[..., half_dim:]
    return jnp.concatenate([first_half * cosine - second_half * sine, second_half * cosine + first_half * sine], axis=-1)

def attend(queries, keys, values, query_pos, key_pos, width):
    scores = jnp.einsum('qgd,kd->gqk', queries.astype(jnp.float32), keys.astype(jnp.float32)) * HD ** (-0.5)
    distance = query_pos[:, None] - key_pos[None, :]
    inside = ((distance >= 0) & (distance < width) & (key_pos[None, :] >= 0))[None]
    scores = jnp.where(inside, scores, jnp.float32(-1e+30))
    highest = lax.optimization_barrier(jnp.max(scores, axis=2, keepdims=True))
    expo = jnp.where(inside, jnp.exp(scores - highest), jnp.float32(0.0))
    probs = (expo / lax.optimization_barrier(jnp.sum(expo, axis=2, keepdims=True))).astype(jnp.bfloat16)
    return jnp.einsum('gqk,kd->qgd', probs.astype(jnp.float32), values.astype(jnp.float32)).astype(jnp.bfloat16)

def normalize(token_rows, gain_row):
    wide_rows = token_rows.astype(jnp.float32)
    mean_square = lax.optimization_barrier(jnp.mean(wide_rows * wide_rows, axis=1, keepdims=True))
    return (wide_rows * lax.rsqrt(mean_square + NORM_EPS) * gain_row.astype(jnp.float32)[None, :]).astype(jnp.bfloat16)

def reference(hidden_in, norm_gain, query_weight, keyval_weight, output_weight, windows):
    positions = jnp.arange(TOKENS, dtype=jnp.int32)
    group = QHEADS // KVHEADS
    blocks = []
    for section in range(N_SEGMENT):
        normed = normalize(hidden_in[section], norm_gain[section])
        key_value = jnp.dot(normed, keyval_weight[section], preferred_element_type=jnp.float32).reshape(TOKENS, KVHEADS, 2, HD)
        keys = rotate(key_value[:, :, 0], positions).astype(jnp.bfloat16)
        values = key_value[:, :, 1].astype(jnp.bfloat16)
        queries = jnp.dot(normed, query_weight[section], preferred_element_type=jnp.float32).reshape(TOKENS, QHEADS, HD)
        queries = rotate(queries, positions).astype(jnp.bfloat16)
        outs_list = []
        for kv_index in range(KVHEADS):
            outs_list.append(attend(queries[:, kv_index * group:(kv_index + 1) * group], keys[:, kv_index], values[:, kv_index], positions, positions, windows[section]))
        attn = jnp.concatenate(outs_list, axis=1).reshape(TOKENS, QHEADS * HD)
        blocks.append(jnp.dot(attn, output_weight[section], preferred_element_type=jnp.float32).astype(jnp.bfloat16))
    stacked = jnp.stack(blocks)
    return jnp.roll(stacked, 1, axis=0)
```

```python
import functools

import jax
import jax.numpy as jnp
import numpy as np
from jax import lax
from jax.experimental import pallas as pl
from jax.experimental.pallas import tpu as pltpu
from jax.sharding import PartitionSpec as P

HD = 128
REACH = 3
NORM_EPS = 1e-05
CHUNKS = 4
VMEM_BYTES = 48 * 1024 * 1024

ANY = pl.BlockSpec(memory_space=pl.ANY)
VMEM = pl.BlockSpec(memory_space=pltpu.VMEM)
SMEM = pl.BlockSpec(memory_space=pltpu.SMEM)


def rotary_tables(tokens):
    half = HD // 2
    inverse = 10000.0 ** (-np.arange(half, dtype=np.float32) / np.float32(half))
    angles = np.arange(tokens, dtype=np.float32)[:, None] * inverse.astype(np.float32)[None, :]
    cosine = np.cos(angles.astype(np.float64)).astype(np.float32)
    sine = np.sin(angles.astype(np.float64)).astype(np.float32)
    return np.concatenate([cosine, cosine, -sine, sine], axis=1)


def turned(head, table):
    return head * table[:, :HD] + pltpu.roll(head, HD // 2, 1) * table[:, HD:]


def table_copy(table_hbm, table, sem):
    rows = table.shape[0]
    first = pl.multiple_of(lax.axis_index("ctx") * rows, 8)
    return pltpu.make_async_copy(table_hbm.at[pl.ds(first, rows)], table, sem)


def column_copies(weight_hbm, weight, sems, width):
    return [
        pltpu.make_async_copy(
            weight_hbm.at[0, :, pl.ds(k * width, width)],
            weight.at[:, pl.ds(k * width, width)],
            sems.at[k],
        )
        for k in range(weight.shape[1] // width)
    ]


def keyval_kernel(
    hidden_hbm, gain_ref, table_hbm, weight_hbm, kv_ref, normed_ref, hidden, table, weight, sems, wsems
):
    hidden_copy = pltpu.make_async_copy(hidden_hbm.at[0], hidden, sems.at[0])
    hidden_copy.start()
    copies = column_copies(weight_hbm, weight, wsems, 2 * HD)
    for copy in copies:
        copy.start()
    tcopy = table_copy(table_hbm, table, sems.at[1])
    tcopy.start()
    hidden_copy.wait()
    rows = hidden.shape[0]
    gain = gain_ref[...].astype(jnp.float32)

    @pl.loop(0, rows // 16)
    def _(at):
        span = pl.ds(pl.multiple_of(at * 16, 16), 16)
        wide = hidden[span, :].astype(jnp.float32)
        square = jnp.mean(wide * wide, axis=1, keepdims=True)
        normed_ref[span, :] = (wide * lax.rsqrt(square + NORM_EPS) * gain).astype(jnp.bfloat16)

    tcopy.wait()
    turn = table[...]
    for k, copy in enumerate(copies):
        copy.wait()
        both = jnp.dot(
            normed_ref[...], weight[:, 2 * HD * k : 2 * HD * (k + 1)], preferred_element_type=jnp.float32
        )
        kv_ref[:, 2 * HD * k : 2 * HD * k + HD] = turned(both[:, :HD], turn).astype(jnp.bfloat16)
        kv_ref[:, 2 * HD * k + HD : 2 * HD * (k + 1)] = both[:, HD:].astype(jnp.bfloat16)


def query_kernel(normed_ref, table_hbm, weight_hbm, query_ref, table, weight, sems, wsems):
    copies = column_copies(weight_hbm, weight, wsems, 2 * HD)
    for copy in copies:
        copy.start()
    tcopy = table_copy(table_hbm, table, sems.at[0])
    tcopy.start()
    tcopy.wait()
    turn = table[...]
    for k, copy in enumerate(copies):
        copy.wait()
        both = jnp.dot(
            normed_ref[...], weight[:, 2 * HD * k : 2 * HD * (k + 1)], preferred_element_type=jnp.float32
        )
        for part in range(2):
            at = 2 * HD * k + HD * part
            query_ref[:, at : at + HD] = turned(both[:, HD * part : HD * (part + 1)], turn).astype(
                jnp.bfloat16
            )


def output_copies(weight_hbm, weight, sems, places, width):
    return [
        pltpu.make_async_copy(
            weight_hbm.at[0, :, pl.ds(pl.multiple_of(place, 128), width)],
            weight.at[:, pl.ds(k * width, width)],
            sems.at[k],
        )
        for k, place in enumerate(places)
    ]


def peer_place(steps, half):
    count = lax.axis_size("tp")
    return lax.rem(lax.axis_index("tp") + steps, count) * half


def attend_kernel(block_count, half, width, *refs):
    window_ref, query_ref = refs[:2]
    kv_refs = refs[2 : 2 + block_count]
    weight_hbm = refs[2 + block_count]
    peers = lax.axis_size("tp") - 1
    attn_ref = refs[3 + block_count]
    send_refs = refs[4 + block_count : 4 + block_count + peers]
    weight, wsems = refs[4 + block_count + peers :]
    copies = output_copies(
        weight_hbm, weight, wsems, [peer_place(d, half) for d in range(1, peers + 1)], width
    )
    for copy in copies:
        copy.start()
    rows = query_ref.shape[0]
    kv_count = kv_refs[0].shape[1] // (2 * HD)
    group = query_ref.shape[1] // HD // kv_count
    ctx = lax.axis_index("ctx")
    twin = ctx + 1 - 2 * lax.rem(ctx, 2)
    blocks = [ctx, twin, ctx - 2, twin - 2, twin - 4][:block_count]
    row = lax.broadcasted_iota(jnp.int32, (rows, rows), 0)
    column = lax.broadcasted_iota(jnp.int32, (rows, rows), 1)
    masks = []
    for block in blocks:
        distance = row - column + (ctx - block) * rows
        masks.append((distance >= 0) & (distance < window_ref[0]) & (block >= 0))
    inside = jnp.concatenate(masks, axis=1)[None]
    for g in range(kv_count):
        queries = jnp.concatenate(
            [query_ref[:, HD * (group * g + h) : HD * (group * g + h + 1)] for h in range(group)], axis=0
        )
        keys = jnp.concatenate([r[:, 2 * HD * g : 2 * HD * g + HD] for r in kv_refs], axis=0)
        values = jnp.concatenate([r[:, 2 * HD * g + HD : 2 * HD * (g + 1)] for r in kv_refs], axis=0)
        scores = lax.dot_general(
            queries, keys, (((1,), (1,)), ((), ())), preferred_element_type=jnp.float32
        ).reshape(group, rows, block_count * rows)
        scores = jnp.where(inside, scores * HD ** (-0.5), jnp.float32(-1e30))
        highest = jnp.max(scores, axis=2, keepdims=True)
        expo = jnp.exp(scores - highest)
        total = jnp.sum(expo, axis=2, keepdims=True)
        probs = (expo * (1.0 / total)).astype(jnp.bfloat16).reshape(group * rows, block_count * rows)
        out = jnp.dot(probs, values, preferred_element_type=jnp.float32).astype(jnp.bfloat16)
        for h in range(group):
            at = HD * (group * g + h)
            attn_ref[:, at : at + HD] = out[h * rows : (h + 1) * rows]
    for d in range(peers):
        copies[d].wait()
        send_refs[d][...] = jnp.dot(
            attn_ref[...], weight[:, d * width : (d + 1) * width], preferred_element_type=jnp.float32
        ).astype(jnp.bfloat16)


def peers_kernel(half, width, chunks, attn_ref, weight_hbm, *refs):
    peers = lax.axis_size("tp") - 1
    count = peers * len(chunks)
    send_refs = refs[:count]
    weight, wsems = refs[count:]
    copies = output_copies(
        weight_hbm,
        weight,
        wsems,
        [peer_place(d, half) + j * width for j in chunks for d in range(1, peers + 1)],
        width,
    )
    for copy in copies:
        copy.start()
    for k in range(count):
        copies[k].wait()
        send_refs[k][...] = jnp.dot(
            attn_ref[...], weight[:, k * width : (k + 1) * width], preferred_element_type=jnp.float32
        ).astype(jnp.bfloat16)


def own_kernel(half, width, attn_ref, weight_hbm, after_ref, own_ref, weight, wsems):
    count = half // width
    copies = output_copies(
        weight_hbm, weight, wsems, [peer_place(0, half) + k * width for k in range(count)], width
    )
    for copy in copies:
        copy.start()
    for k in range(count):
        copies[k].wait()
        own_ref[:, k * width : (k + 1) * width] = jnp.dot(
            attn_ref[...], weight[:, k * width : (k + 1) * width], preferred_element_type=jnp.float32
        )


def call(kernel, name, outs, in_specs, scratch, flops, moved):
    return pl.pallas_call(
        kernel,
        out_shape=outs,
        in_specs=in_specs,
        out_specs=jax.tree.map(lambda _: VMEM, outs),
        scratch_shapes=scratch,
        compiler_params=pltpu.CompilerParams(vmem_limit_bytes=VMEM_BYTES),
        cost_estimate=pl.CostEstimate(flops=flops, bytes_accessed=moved, transcendentals=0),
        name=name,
    )


def moved_by(value, axis, steps):
    count = lax.axis_size(axis)
    return lax.ppermute(value, axis, [(source, (source + steps) % count) for source in range(count)])


def twins(value):
    count = lax.axis_size("ctx")
    return lax.ppermute(value, "ctx", [(source, source ^ 1) for source in range(count)])


def body(hidden_in, norm_gain, query_weight, keyval_weight, output_weight, windows):
    bf16, f32 = jnp.bfloat16, jnp.float32
    dma = pltpu.SemaphoreType.DMA
    _, rows, features = hidden_in.shape
    query_columns = query_weight.shape[2]
    kv_columns = keyval_weight.shape[2]
    ctx_count = lax.axis_size("ctx")
    tp_count = lax.axis_size("tp")
    assert ctx_count % 2 == 0
    table = jnp.asarray(rotary_tables(rows * ctx_count))
    own_kv, normed = call(
        keyval_kernel,
        "keyval",
        (jax.ShapeDtypeStruct((rows, kv_columns), bf16), jax.ShapeDtypeStruct((rows, features), bf16)),
        [ANY, VMEM, ANY, ANY],
        [
            pltpu.VMEM((rows, features), bf16),
            pltpu.VMEM((rows, 2 * HD), f32),
            pltpu.VMEM((features, kv_columns), bf16),
            dma((2,)),
            dma((kv_columns // (2 * HD),)),
        ],
        2 * rows * features * kv_columns,
        2 * features * kv_columns,
    )(hidden_in, norm_gain, table, keyval_weight)
    behind = moved_by(own_kv, "ctx", 2)
    beside = twins(own_kv)
    queries = call(
        query_kernel,
        "query",
        jax.ShapeDtypeStruct((rows, query_columns), bf16),
        [VMEM, ANY, ANY],
        [
            pltpu.VMEM((rows, 2 * HD), f32),
            pltpu.VMEM((features, query_columns), bf16),
            dma((1,)),
            dma((query_columns // (2 * HD),)),
        ],
        2 * rows * features * query_columns,
        2 * features * query_columns,
    )(normed, table, query_weight)
    behind_beside = twins(behind)
    kv_list = [own_kv, beside, behind, behind_beside]
    if ctx_count > 4:
        kv_list.append(moved_by(behind_beside, "ctx", 2))
    out_columns = output_weight.shape[2]
    half = out_columns // tp_count
    width = half // CHUNKS
    peers = tp_count - 1
    send = jax.ShapeDtypeStruct((rows, width), bf16)
    attn, *first = call(
        functools.partial(attend_kernel, len(kv_list), half, width),
        "attend",
        [jax.ShapeDtypeStruct((rows, query_columns), bf16)] + [send] * peers,
        [SMEM, VMEM] + [VMEM] * len(kv_list) + [ANY],
        [pltpu.VMEM((query_columns, peers * width), bf16), dma((peers,))],
        2 * rows * query_columns * width,
        2 * query_columns * width,
    )(windows, queries, *kv_list, output_weight)
    later = range(1, CHUNKS)
    rest = call(
        functools.partial(peers_kernel, half, width, later),
        "peers",
        [send] * (peers * len(later)),
        [VMEM, ANY],
        [pltpu.VMEM((query_columns, peers * len(later) * width), bf16), dma((peers * len(later),))],
        2 * rows * query_columns * width * len(later) * peers,
        2 * query_columns * width * len(later) * peers,
    )(attn, output_weight)
    own = call(
        functools.partial(own_kernel, half, width),
        "own",
        jax.ShapeDtypeStruct((rows, half), f32),
        [VMEM, ANY, ANY],
        [pltpu.VMEM((query_columns, half), bf16), dma((CHUNKS,))],
        2 * rows * query_columns * half,
        2 * query_columns * half,
    )(attn, output_weight, rest[-1])
    sends = list(first) + list(rest)
    pieces = []
    for j in range(CHUNKS):
        total = own[:, j * width : (j + 1) * width]
        for d in range(peers):
            total = total + moved_by(sends[j * peers + d], "tp", d + 1).astype(f32)
        pieces.append(moved_by(total.astype(bf16), "segment", 1))
    return jnp.concatenate(pieces, axis=1)[None]


def solution(mesh):
    in_specs = (
        P("segment", "ctx", None),
        P("segment", None),
        P("segment", None, "tp"),
        P("segment", None, "tp"),
        P("segment", "tp", None),
        P("segment"),
    )
    out_specs = P("segment", "ctx", "tp")
    return jax.shard_map(body, mesh=mesh, in_specs=in_specs, out_specs=out_specs, check_vma=False)
```

```python
import functools

import jax
import jax.numpy as jnp
import numpy as np
from jax import lax
from jax.experimental import pallas as pl
from jax.experimental.pallas import tpu as pltpu
from jax.sharding import PartitionSpec as P

HD = 128
REACH = 3
NORM_EPS = 1e-05
CHUNKS = 4
MIB = 1024 * 1024

HBM = pl.BlockSpec(memory_space=pltpu.HBM)
VMEM = pl.BlockSpec(memory_space=pltpu.VMEM)
SMEM = pl.BlockSpec(memory_space=pltpu.SMEM)


def rotary_tables(tokens):
    half = HD // 2
    inverse = 10000.0 ** (-np.arange(half, dtype=np.float32) / np.float32(half))
    angles = np.arange(tokens, dtype=np.float32)[:, None] * inverse.astype(np.float32)[None, :]
    cosine = np.cos(angles.astype(np.float64)).astype(np.float32)
    sine = np.sin(angles.astype(np.float64)).astype(np.float32)
    return np.concatenate([cosine, cosine, -sine, sine], axis=1)


def turned(head, table):
    return head * table[:, :HD] + pltpu.roll(head, HD // 2, 1) * table[:, HD:]


def table_copy(table_hbm, table, sem):
    rows = table.shape[0]
    first = pl.multiple_of(lax.axis_index("ctx") * rows, 8)
    return pltpu.make_async_copy(table_hbm.at[pl.ds(first, rows)], table, sem)


def column_copies(weight_hbm, weight, sems, width):
    return [
        pltpu.make_async_copy(
            weight_hbm.at[0, :, pl.ds(k * width, width)],
            weight.at[:, pl.ds(k * width, width)],
            sems.at[k],
        )
        for k in range(weight.shape[1] // width)
    ]


def keyval_kernel(
    hidden_hbm, gain_hbm, table_hbm, weight_hbm, kv_ref, normed_ref, table, hidden, gain, weight, sems, wsems
):
    hidden_copy = pltpu.make_async_copy(hidden_hbm.at[0], hidden, sems.at[0])
    hidden_copy.start()
    gain_copy = pltpu.make_async_copy(gain_hbm, gain, sems.at[2])
    gain_copy.start()
    copies = column_copies(weight_hbm, weight, wsems, 2 * HD)
    for copy in copies:
        copy.start()
    tcopy = table_copy(table_hbm, table, sems.at[1])
    tcopy.start()
    hidden_copy.wait()
    gain_copy.wait()
    rows = hidden.shape[0]
    scale = gain[...].astype(jnp.float32)

    @pl.loop(0, rows // 16)
    def _(at):
        span = pl.ds(pl.multiple_of(at * 16, 16), 16)
        wide = hidden[span, :].astype(jnp.float32)
        square = jnp.mean(wide * wide, axis=1, keepdims=True)
        normed_ref[span, :] = (wide * lax.rsqrt(square + NORM_EPS) * scale).astype(jnp.bfloat16)

    tcopy.wait()
    turn = table[...]
    for k, copy in enumerate(copies):
        copy.wait()
        both = jnp.dot(
            normed_ref[...], weight[:, 2 * HD * k : 2 * HD * (k + 1)], preferred_element_type=jnp.float32
        )
        kv_ref[:, 2 * HD * k : 2 * HD * k + HD] = turned(both[:, :HD], turn).astype(jnp.bfloat16)
        kv_ref[:, 2 * HD * k + HD : 2 * HD * (k + 1)] = both[:, HD:].astype(jnp.bfloat16)


def query_kernel(normed_ref, table, weight_hbm, query_ref, weight, wsems):
    copies = column_copies(weight_hbm, weight, wsems, 2 * HD)
    for copy in copies:
        copy.start()
    turn = table[...]
    for k, copy in enumerate(copies):
        copy.wait()
        both = jnp.dot(
            normed_ref[...], weight[:, 2 * HD * k : 2 * HD * (k + 1)], preferred_element_type=jnp.float32
        )
        for part in range(2):
            at = 2 * HD * k + HD * part
            query_ref[:, at : at + HD] = turned(both[:, HD * part : HD * (part + 1)], turn).astype(
                jnp.bfloat16
            )


def output_copies(weight_hbm, weight, sems, places, width):
    return [
        pltpu.make_async_copy(
            weight_hbm.at[0, :, pl.ds(pl.multiple_of(place, 128), width)],
            weight.at[:, pl.ds(k * width, width)],
            sems.at[k],
        )
        for k, place in enumerate(places)
    ]


def peer_place(steps, half):
    count = lax.axis_size("tp")
    return lax.rem(lax.axis_index("tp") + steps, count) * half


def attend_kernel(block_count, half, width, *refs):
    window_ref, query_ref = refs[:2]
    kv_refs = refs[2 : 2 + block_count]
    weight_hbm = refs[2 + block_count]
    peers = lax.axis_size("tp") - 1
    attn_ref = refs[3 + block_count]
    send_refs = refs[4 + block_count : 4 + block_count + peers]
    weight, wsems = refs[4 + block_count + peers :]
    copies = output_copies(
        weight_hbm, weight, wsems, [peer_place(d, half) for d in range(1, peers + 1)], width
    )
    for copy in copies:
        copy.start()
    rows = query_ref.shape[0]
    kv_count = kv_refs[0].shape[1] // (2 * HD)
    group = query_ref.shape[1] // HD // kv_count
    ctx = lax.axis_index("ctx")
    twin = ctx + 1 - 2 * lax.rem(ctx, 2)
    blocks = [ctx, twin, ctx - 2, twin - 2, twin - 4][:block_count]
    row = lax.broadcasted_iota(jnp.int32, (rows, rows), 0)
    column = lax.broadcasted_iota(jnp.int32, (rows, rows), 1)
    masks = []
    for block in blocks:
        distance = row - column + (ctx - block) * rows
        masks.append((distance >= 0) & (distance < window_ref[0]) & (block >= 0))
    inside = jnp.concatenate(masks, axis=1)[None]
    for g in range(kv_count):
        queries = jnp.concatenate(
            [query_ref[:, HD * (group * g + h) : HD * (group * g + h + 1)] for h in range(group)], axis=0
        )
        keys = jnp.concatenate([r[:, 2 * HD * g : 2 * HD * g + HD] for r in kv_refs], axis=0)
        values = jnp.concatenate([r[:, 2 * HD * g + HD : 2 * HD * (g + 1)] for r in kv_refs], axis=0)
        scores = lax.dot_general(
            queries, keys, (((1,), (1,)), ((), ())), preferred_element_type=jnp.float32
        ).reshape(group, rows, block_count * rows)
        scores = jnp.where(inside, scores * HD ** (-0.5), jnp.float32(-1e30))
        highest = jnp.max(scores, axis=2, keepdims=True)
        expo = jnp.exp(scores - highest)
        total = jnp.sum(expo, axis=2, keepdims=True)
        probs = (expo * (1.0 / total)).astype(jnp.bfloat16).reshape(group * rows, block_count * rows)
        out = jnp.dot(probs, values, preferred_element_type=jnp.float32).astype(jnp.bfloat16)
        for h in range(group):
            at = HD * (group * g + h)
            attn_ref[:, at : at + HD] = out[h * rows : (h + 1) * rows]
    for d in range(peers):
        copies[d].wait()
        send_refs[d][...] = jnp.dot(
            attn_ref[...], weight[:, d * width : (d + 1) * width], preferred_element_type=jnp.float32
        ).astype(jnp.bfloat16)


def peers_kernel(half, width, chunks, attn_ref, weight_hbm, *refs):
    peers = lax.axis_size("tp") - 1
    count = peers * len(chunks)
    send_refs = refs[:count]
    weight, wsems = refs[count:]
    copies = output_copies(
        weight_hbm,
        weight,
        wsems,
        [peer_place(d, half) + j * width for j in chunks for d in range(1, peers + 1)],
        width,
    )
    for copy in copies:
        copy.start()
    for k in range(count):
        copies[k].wait()
        send_refs[k][...] = jnp.dot(
            attn_ref[...], weight[:, k * width : (k + 1) * width], preferred_element_type=jnp.float32
        ).astype(jnp.bfloat16)


def own_kernel(half, width, attn_ref, weight_hbm, after_ref, *refs):
    count = half // width
    own_refs = refs[:count]
    weight, wsems = refs[count:]
    copies = output_copies(
        weight_hbm, weight, wsems, [peer_place(0, half) + k * width for k in range(count)], width
    )
    for copy in copies:
        copy.start()
    for k in range(count):
        copies[k].wait()
        own_refs[k][...] = jnp.dot(
            attn_ref[...], weight[:, k * width : (k + 1) * width], preferred_element_type=jnp.float32
        )


def add_kernel(own_ref, *refs):
    total = own_ref[...]
    for peer_ref in refs[: lax.axis_size("tp") - 1]:
        total = total + peer_ref[...].astype(jnp.float32)
    refs[-1][...] = total.astype(jnp.bfloat16)


def call(kernel, name, outs, in_specs, scratch, mib, flops=0, moved=0):
    return pl.pallas_call(
        kernel,
        out_shape=outs,
        in_specs=in_specs,
        out_specs=jax.tree.map(lambda _: VMEM, outs),
        scratch_shapes=scratch,
        compiler_params=pltpu.CompilerParams(vmem_limit_bytes=mib * MIB),
        cost_estimate=pl.CostEstimate(flops=flops, bytes_accessed=moved, transcendentals=0),
        name=name,
    )


def moved_by(value, axis, steps):
    count = lax.axis_size(axis)
    return lax.ppermute(value, axis, [(source, (source + steps) % count) for source in range(count)])


def twins(value):
    count = lax.axis_size("ctx")
    return lax.ppermute(value, "ctx", [(source, source ^ 1) for source in range(count)])


def body(hidden_in, norm_gain, query_weight, keyval_weight, output_weight, windows):
    bf16, f32 = jnp.bfloat16, jnp.float32
    dma = pltpu.SemaphoreType.DMA
    _, rows, features = hidden_in.shape
    query_columns = query_weight.shape[2]
    kv_columns = keyval_weight.shape[2]
    ctx_count = lax.axis_size("ctx")
    tp_count = lax.axis_size("tp")
    assert ctx_count % 2 == 0
    table = jnp.asarray(rotary_tables(rows * ctx_count))
    hidden_in, norm_gain, table, query_weight, keyval_weight, output_weight = (
        pltpu.with_memory_space_constraint(value, pltpu.HBM)
        for value in (hidden_in, norm_gain, table, query_weight, keyval_weight, output_weight)
    )
    own_kv, normed, turns = call(
        keyval_kernel,
        "keyval",
        (
            jax.ShapeDtypeStruct((rows, kv_columns), bf16),
            jax.ShapeDtypeStruct((rows, features), bf16),
            jax.ShapeDtypeStruct((rows, 2 * HD), f32),
        ),
        [HBM, HBM, HBM, HBM],
        [
            pltpu.VMEM((rows, features), bf16),
            pltpu.VMEM((1, features), bf16),
            pltpu.VMEM((features, kv_columns), bf16),
            dma((3,)),
            dma((kv_columns // (2 * HD),)),
        ],
        48,
        2 * rows * features * kv_columns,
        2 * features * kv_columns,
    )(hidden_in, norm_gain, table, keyval_weight)
    behind = moved_by(own_kv, "ctx", 2)
    beside = twins(own_kv)
    queries = call(
        query_kernel,
        "query",
        jax.ShapeDtypeStruct((rows, query_columns), bf16),
        [VMEM, VMEM, HBM],
        [
            pltpu.VMEM((features, query_columns), bf16),
            dma((query_columns // (2 * HD),)),
        ],
        48,
        2 * rows * features * query_columns,
        2 * features * query_columns,
    )(normed, turns, query_weight)
    behind, queries = lax.optimization_barrier((behind, queries))
    behind_beside = twins(behind)
    kv_list = [own_kv, beside, behind, behind_beside]
    if ctx_count > 4:
        kv_list.append(moved_by(behind_beside, "ctx", 2))
    out_columns = output_weight.shape[2]
    half = out_columns // tp_count
    width = half // CHUNKS
    peers = tp_count - 1
    send = jax.ShapeDtypeStruct((rows, width), bf16)
    attn, *first = call(
        functools.partial(attend_kernel, len(kv_list), half, width),
        "attend",
        [jax.ShapeDtypeStruct((rows, query_columns), bf16)] + [send] * peers,
        [SMEM, VMEM] + [VMEM] * len(kv_list) + [HBM],
        [pltpu.VMEM((query_columns, peers * width), bf16), dma((peers,))],
        48,
    )(windows, queries, *kv_list, output_weight)
    later = range(1, CHUNKS)
    rest = call(
        functools.partial(peers_kernel, half, width, later),
        "peers",
        [send] * (peers * len(later)),
        [VMEM, HBM],
        [pltpu.VMEM((query_columns, peers * len(later) * width), bf16), dma((peers * len(later),))],
        48,
    )(attn, output_weight)
    own = call(
        functools.partial(own_kernel, half, width),
        "own",
        [jax.ShapeDtypeStruct((rows, width), f32)] * CHUNKS,
        [VMEM, HBM, VMEM],
        [pltpu.VMEM((query_columns, half), bf16), dma((CHUNKS,))],
        48,
    )(attn, output_weight, rest[-1])
    sends = list(first) + list(rest)
    pieces = []
    totals = []
    came = [
        [moved_by(sends[j * peers + d], "tp", d + 1) for d in range(peers)] for j in range(CHUNKS)
    ]
    for j in range(CHUNKS):
        parts = [own[j]] + came[j] + pieces[max(0, j - 2) : max(0, j - 1)] + totals[-1:]
        total = call(
            add_kernel, "add", send, [VMEM] * len(parts), [], 16
        )(*parts)
        totals.append(total)
        pieces.append(moved_by(total, "segment", 1))
    return jnp.concatenate(pieces, axis=1)[None]


def solution(mesh):
    in_specs = (
        P("segment", "ctx", None),
        P("segment", None),
        P("segment", None, "tp"),
        P("segment", None, "tp"),
        P("segment", "tp", None),
        P("segment"),
    )
    out_specs = P("segment", "ctx", "tp")
    return jax.shard_map(body, mesh=mesh, in_specs=in_specs, out_specs=out_specs, check_vma=False)
```

```python
import functools

import jax
import jax.numpy as jnp
import numpy as np
from jax import lax
from jax.experimental import pallas as pl
from jax.experimental.pallas import tpu as pltpu
from jax.sharding import PartitionSpec as P

HD = 128
REACH = 3
NORM_EPS = 1e-05
SHARES = (5, 6, 5)
LOG2E = 1.4426950408889634
MIB = 1024 * 1024

HBM = pl.BlockSpec(memory_space=pltpu.HBM)
VMEM = pl.BlockSpec(memory_space=pltpu.VMEM)
SMEM = pl.BlockSpec(memory_space=pltpu.SMEM)


def rotary_tables(tokens):
    half = HD // 2
    inverse = 10000.0 ** (-np.arange(half, dtype=np.float32) / np.float32(half))
    angles = np.arange(tokens, dtype=np.float32)[:, None] * inverse.astype(np.float32)[None, :]
    cosine = np.cos(angles.astype(np.float64)).astype(np.float32)
    sine = np.sin(angles.astype(np.float64)).astype(np.float32)
    return np.concatenate([cosine, cosine, -sine, sine], axis=1)


def turned(head, table):
    return head * table[:, :HD] + pltpu.roll(head, HD // 2, 1) * table[:, HD:]


def table_copy(table_hbm, table, sem):
    rows = table.shape[0]
    first = pl.multiple_of(lax.axis_index("ctx") * rows, 8)
    return pltpu.make_async_copy(table_hbm.at[pl.ds(first, rows)], table, sem)


def column_copies(weight_hbm, weight, sems):
    width = weight.shape[1] // sems.shape[0]
    return [
        pltpu.make_async_copy(
            weight_hbm.at[0, :, pl.ds(k * width, width)],
            weight.at[:, pl.ds(k * width, width)],
            sems.at[k],
        )
        for k in range(sems.shape[0])
    ]


def keyval_kernel(
    hidden_hbm, gain_hbm, table_hbm, weight_hbm, kv_ref, normed_ref, table, hidden, gain, weight, sems, wsems
):
    hidden_copy = pltpu.make_async_copy(hidden_hbm.at[0], hidden, sems.at[0])
    hidden_copy.start()
    gain_copy = pltpu.make_async_copy(gain_hbm, gain, sems.at[2])
    gain_copy.start()
    tcopy = table_copy(table_hbm, table, sems.at[1])
    tcopy.start()
    copies = column_copies(weight_hbm, weight, wsems)
    for copy in copies:
        copy.start(priority=1)
    gain_copy.wait()
    hidden_copy.wait()
    rows, features = hidden.shape
    spans = [slice(at, at + HD) for at in range(0, features, HD)]
    squares = jnp.zeros((rows, HD), jnp.float32)
    for span in spans:
        wide = hidden[:, span].astype(jnp.float32)
        squares = squares + wide * wide
    mean = jnp.sum(squares, axis=1, keepdims=True) * (1.0 / features)
    inverse = jnp.broadcast_to(lax.rsqrt(mean + NORM_EPS), (rows, HD))
    for span in spans:
        wide = hidden[:, span].astype(jnp.float32)
        normed_ref[:, span] = (wide * inverse * gain[:, span].astype(jnp.float32)).astype(jnp.bfloat16)
    tcopy.wait()
    turn = table[...]
    width = weight.shape[1] // len(copies)
    for k, copy in enumerate(copies):
        copy.wait()
        both = jnp.dot(
            normed_ref[...], weight[:, width * k : width * (k + 1)], preferred_element_type=jnp.float32
        )
        for part in range(0, width, 2 * HD):
            at = width * k + part
            kv_ref[:, at : at + HD] = turned(both[:, part : part + HD], turn).astype(jnp.bfloat16)
            kv_ref[:, at + HD : at + 2 * HD] = both[:, part + HD : part + 2 * HD].astype(jnp.bfloat16)


def query_kernel(normed_ref, table, weight_hbm, query_ref, weight, wsems):
    copies = column_copies(weight_hbm, weight, wsems)
    for copy in copies:
        copy.start()
    turn = table[...]
    width = weight.shape[1] // len(copies)
    for k, copy in enumerate(copies):
        copy.wait()
        both = jnp.dot(
            normed_ref[...], weight[:, width * k : width * (k + 1)], preferred_element_type=jnp.float32
        )
        for part in range(0, width, HD):
            at = width * k + part
            query_ref[:, at : at + HD] = turned(both[:, part : part + HD], turn).astype(jnp.bfloat16)


def output_copies(weight_hbm, weights, sems, places):
    return [
        pltpu.make_async_copy(
            weight_hbm.at[0, :, pl.ds(pl.multiple_of(place, 128), weight.shape[1])], weight, sems.at[k]
        )
        for k, (weight, place) in enumerate(zip(weights, places))
    ]


def peer_place(steps, half, start):
    count = lax.axis_size("tp")
    return lax.rem(lax.axis_index("tp") + steps, count) * half + start


def steps_of(width):
    return [(at, min(256, width - at)) for at in range(0, width, 256)]


def multiply(attn_ref, weight_ref, out_ref):
    for at, step in steps_of(weight_ref.shape[1]):
        out_ref[:, at : at + step] = jnp.dot(
            attn_ref[...], weight_ref[:, at : at + step], preferred_element_type=jnp.float32
        ).astype(out_ref.dtype)


def attend_kernel(block_count, places, window_ref, query_ref, *refs):
    kv_refs, weight_hbm, refs = refs[:block_count], refs[block_count], refs[block_count + 1 :]
    peers = lax.axis_size("tp") - 1
    attn_ref, send_refs, kept_refs = refs[0], refs[1 : peers + 1], refs[peers + 1 : -peers - 1]
    weights, sems = refs[-peers - 1 : -1], refs[-1]
    copies = output_copies(weight_hbm, weights + kept_refs, sems, [peer_place(*p) for p in places])
    for copy in copies:
        copy.start()
    rows = query_ref.shape[0]
    kv_count = kv_refs[0].shape[1] // (2 * HD)
    group = query_ref.shape[1] // HD // kv_count
    ctx = lax.axis_index("ctx")
    twin = ctx + 1 - 2 * lax.rem(ctx, 2)
    row = lax.broadcasted_iota(jnp.int32, (rows, rows), 0)
    column = lax.broadcasted_iota(jnp.int32, (rows, rows), 1)
    masks = []
    for block in [ctx, twin, ctx - 2, twin - 2, twin - 4][:block_count]:
        distance = row - column + (ctx - block) * rows
        masks.append((distance >= 0) & (distance < window_ref[0]) & (block >= 0))
    inside = jnp.concatenate(masks, axis=1)[None]
    for g in range(kv_count):
        queries = jnp.concatenate(
            [query_ref[:, HD * (group * g + h) : HD * (group * g + h + 1)] for h in range(group)], axis=0
        )
        keys = jnp.concatenate([r[:, 2 * HD * g : 2 * HD * g + HD] for r in kv_refs], axis=0)
        values = jnp.concatenate([r[:, 2 * HD * g + HD : 2 * HD * (g + 1)] for r in kv_refs], axis=0)
        scores = lax.dot_general(
            queries, keys, (((1,), (1,)), ((), ())), preferred_element_type=jnp.float32
        ).reshape(group, rows, block_count * rows)
        scores = jnp.where(inside, scores * (HD ** (-0.5) * LOG2E), jnp.float32(-1e30))
        highest = jnp.max(scores, axis=2, keepdims=True)
        expo = jnp.exp2(scores - highest).astype(jnp.bfloat16).reshape(group * rows, block_count * rows)
        sums = jnp.dot(
            expo, jnp.concatenate([values, jnp.ones_like(values)], axis=1), preferred_element_type=jnp.float32
        )
        out = (sums[:, :HD] * (1.0 / sums[:, HD:])).astype(jnp.bfloat16)
        for h in range(group):
            at = HD * (group * g + h)
            attn_ref[:, at : at + HD] = out[h * rows : (h + 1) * rows]
    for copy, weight, send_ref in zip(copies, weights, send_refs):
        copy.wait()
        multiply(attn_ref, weight, send_ref)
    for copy in copies[peers:]:
        copy.wait()


def multiply_kernel(held, places, attn_ref, *refs):
    held_refs, weight_hbm, refs = refs[:held], refs[held], refs[held + 2 :]
    count = held + len(places)
    out_refs, weights = refs[:count], refs[count : count + len(places)]
    pieces = [
        (k, at, step) for k, weight in enumerate(weights) for at, step in steps_of(weight.shape[1])
    ]
    copies = []
    if places:
        copies = output_copies(
            weight_hbm,
            [weights[k].at[:, pl.ds(at, step)] for k, at, step in pieces],
            refs[-1],
            [peer_place(*places[k]) + at for k, at, _ in pieces],
        )
    for copy in copies:
        copy.start()
    for weight_ref, out_ref in zip(held_refs, out_refs):
        multiply(attn_ref, weight_ref, out_ref)
    for copy, (k, at, step) in zip(copies, pieces):
        copy.wait()
        out_ref = out_refs[held + k]
        out_ref[:, at : at + step] = jnp.dot(
            attn_ref[...], weights[k][:, at : at + step], preferred_element_type=jnp.float32
        ).astype(out_ref.dtype)


def add_kernel(own_ref, *refs):
    total = own_ref[...]
    for peer_ref in refs[: lax.axis_size("tp") - 1]:
        total = total + peer_ref[...].astype(jnp.float32)
    refs[-1][...] = total.astype(jnp.bfloat16)


def call(kernel, name, outs, in_specs, scratch, mib, flops=0, moved=0):
    return pl.pallas_call(
        kernel,
        out_shape=outs,
        in_specs=in_specs,
        out_specs=jax.tree.map(lambda _: VMEM, outs),
        scratch_shapes=scratch,
        compiler_params=pltpu.CompilerParams(vmem_limit_bytes=mib * MIB),
        cost_estimate=pl.CostEstimate(flops=flops, bytes_accessed=moved, transcendentals=0),
        name=name,
    )


def moved_by(value, axis, steps):
    count = lax.axis_size(axis)
    return lax.ppermute(value, axis, [(source, (source + steps) % count) for source in range(count)])


def twins(value):
    count = lax.axis_size("ctx")
    return lax.ppermute(value, "ctx", [(source, source ^ 1) for source in range(count)])


def body(hidden_in, norm_gain, query_weight, keyval_weight, output_weight, windows):
    bf16, f32 = jnp.bfloat16, jnp.float32
    dma = pltpu.SemaphoreType.DMA
    _, rows, features = hidden_in.shape
    query_columns = query_weight.shape[2]
    kv_columns = keyval_weight.shape[2]
    ctx_count = lax.axis_size("ctx")
    tp_count = lax.axis_size("tp")
    assert ctx_count % 2 == 0
    table = jnp.asarray(rotary_tables(rows * ctx_count))
    hidden_in, norm_gain, table, query_weight, keyval_weight, output_weight = (
        pltpu.with_memory_space_constraint(value, pltpu.HBM)
        for value in (hidden_in, norm_gain, table, query_weight, keyval_weight, output_weight)
    )
    own_kv, normed, turns = call(
        keyval_kernel,
        "keyval",
        (
            jax.ShapeDtypeStruct((rows, kv_columns), bf16),
            jax.ShapeDtypeStruct((rows, features), bf16),
            jax.ShapeDtypeStruct((rows, 2 * HD), f32),
        ),
        [HBM, HBM, HBM, HBM],
        [
            pltpu.VMEM((rows, features), bf16),
            pltpu.VMEM((1, features), bf16),
            pltpu.VMEM((features, kv_columns), bf16),
            dma((3,)),
            dma((max(1, kv_columns // 512),)),
        ],
        48,
        2 * rows * features * kv_columns,
        2 * features * kv_columns,
    )(hidden_in, norm_gain, table, keyval_weight)
    behind = moved_by(own_kv, "ctx", 2)
    beside = twins(own_kv)
    queries = call(
        query_kernel,
        "query",
        jax.ShapeDtypeStruct((rows, query_columns), bf16),
        [VMEM, VMEM, HBM],
        [
            pltpu.VMEM((features, query_columns), bf16),
            dma((max(1, query_columns // 512),)),
        ],
        48,
        2 * rows * features * query_columns,
        2 * features * query_columns,
    )(normed, turns, query_weight)
    behind, queries = lax.optimization_barrier((behind, queries))
    behind_beside = twins(behind)
    kv_list = [own_kv, beside, behind, behind_beside]
    if ctx_count > 4:
        kv_list.append(moved_by(behind_beside, "ctx", 2))
    out_columns = output_weight.shape[2]
    half = out_columns // tp_count
    peers = tp_count - 1
    cuts = [half * sum(SHARES[:j]) // sum(SHARES) // 128 * 128 for j in range(len(SHARES) + 1)]
    widths = [end - start for start, end in zip(cuts, cuts[1:])]
    sends = [[jax.ShapeDtypeStruct((rows, width), bf16)] * peers for width in widths]
    owns = [jax.ShapeDtypeStruct((rows, width), f32) for width in widths]

    def away(j):
        return [(d, half, cuts[j]) for d in range(1, peers + 1)]

    def here(j):
        return [(0, half, cuts[j])]

    def weights_of(j):
        return jax.ShapeDtypeStruct((query_columns, widths[j]), bf16)

    def products(name, outs, attn, held, places, columns, after):
        return call(
            functools.partial(multiply_kernel, len(held), places),
            name,
            outs,
            [VMEM] * (1 + len(held)) + [HBM, VMEM],
            [pltpu.VMEM((query_columns, width), bf16) for width in columns]
            + ([dma((sum(len(steps_of(width)) for width in columns),))] if places else []),
            40,
        )(attn, *held, output_weight, after)

    kept = [weights_of(1)] * peers + [weights_of(0)]
    attn, *made = call(
        functools.partial(attend_kernel, len(kv_list), away(0) + away(1) + here(0)),
        "attend",
        [jax.ShapeDtypeStruct((rows, query_columns), bf16)] + sends[0] + kept,
        [SMEM, VMEM] + [VMEM] * len(kv_list) + [HBM],
        [pltpu.VMEM((query_columns, widths[0]), bf16)] * peers + [dma((2 * peers + 1,))],
        40,
    )(windows, queries, *kv_list, output_weight)
    sent = [made[:peers]]
    sent.append(products("away1", sends[1], attn, made[peers : 2 * peers], [], [], made[0]))
    own, *last = products(
        "own0", owns[:1] + sends[2], attn, made[-1:], away(2), [widths[2]] * peers, sent[1][0]
    )
    sent.append(last)
    came = [[moved_by(value, "tp", d + 1) for d, value in enumerate(values)] for values in sent]
    pieces, totals = [], []
    for j in range(len(widths)):
        parts = [own] + came[j] + pieces[max(0, j - 2) : max(0, j - 1)] + totals[-1:]
        total = call(add_kernel, "add", sends[j][0], [VMEM] * len(parts), [], 16)(*parts)
        totals.append(total)
        pieces.append(moved_by(total, "segment", 1))
        if j + 1 < len(widths):
            (own,) = products("own", owns[j + 1 : j + 2], attn, [], here(j + 1), widths[j + 1 : j + 2], total)
    return jnp.concatenate(pieces, axis=1)[None]


def solution(mesh):
    in_specs = (
        P("segment", "ctx", None),
        P("segment", None),
        P("segment", None, "tp"),
        P("segment", None, "tp"),
        P("segment", "tp", None),
        P("segment"),
    )
    out_specs = P("segment", "ctx", "tp")
    return jax.shard_map(body, mesh=mesh, in_specs=in_specs, out_specs=out_specs, check_vma=False)
```

```python
import functools

import jax
import jax.numpy as jnp
import numpy as np
from jax import lax
from jax.experimental import pallas as pl
from jax.experimental.pallas import tpu as pltpu
from jax.sharding import PartitionSpec as P

HD = 128
REACH = 3
NORM_EPS = 1e-05
SHARES = (5, 6, 5)
LOG2E = 1.4426950408889634
MIB = 1024 * 1024

HBM = pl.BlockSpec(memory_space=pltpu.HBM)
VMEM = pl.BlockSpec(memory_space=pltpu.VMEM)
SMEM = pl.BlockSpec(memory_space=pltpu.SMEM)


def rotary_tables(tokens):
    half = HD // 2
    inverse = 10000.0 ** (-np.arange(half, dtype=np.float32) / np.float32(half))
    angles = np.arange(tokens, dtype=np.float32)[:, None] * inverse.astype(np.float32)[None, :]
    cosine = np.cos(angles.astype(np.float64)).astype(np.float32)
    sine = np.sin(angles.astype(np.float64)).astype(np.float32)
    return np.concatenate([cosine, cosine, -sine, sine], axis=1)


def turned(head, table):
    return head * table[:, :HD] + pltpu.roll(head, HD // 2, 1) * table[:, HD:]


def table_copy(table_hbm, table, sem):
    rows = table.shape[0]
    first = pl.multiple_of(lax.axis_index("ctx") * rows, 8)
    return pltpu.make_async_copy(table_hbm.at[pl.ds(first, rows)], table, sem)


def column_copies(weight_hbm, weight, sems):
    width = weight.shape[1] // sems.shape[0]
    return [
        pltpu.make_async_copy(
            weight_hbm.at[0, :, pl.ds(k * width, width)],
            weight.at[:, pl.ds(k * width, width)],
            sems.at[k],
        )
        for k in range(sems.shape[0])
    ]


def keyval_kernel(
    hidden_hbm, gain_hbm, table_hbm, weight_hbm, kv_ref, normed_ref, table, hidden, gain, weight, sems, wsems
):
    hidden_copy = pltpu.make_async_copy(hidden_hbm.at[0], hidden, sems.at[0])
    hidden_copy.start()
    gain_copy = pltpu.make_async_copy(gain_hbm, gain, sems.at[2])
    gain_copy.start()
    tcopy = table_copy(table_hbm, table, sems.at[1])
    tcopy.start()
    copies = column_copies(weight_hbm, weight, wsems)
    for copy in copies:
        copy.start(priority=1)
    gain_copy.wait()
    hidden_copy.wait()
    rows, features = hidden.shape
    spans = [slice(at, at + HD) for at in range(0, features, HD)]
    squares = jnp.zeros((rows, HD), jnp.float32)
    for span in spans:
        wide = hidden[:, span].astype(jnp.float32)
        squares = squares + wide * wide
    mean = jnp.sum(squares, axis=1, keepdims=True) * (1.0 / features)
    inverse = jnp.broadcast_to(lax.rsqrt(mean + NORM_EPS), (rows, HD))
    for span in spans:
        wide = hidden[:, span].astype(jnp.float32)
        normed_ref[:, span] = (wide * inverse * gain[:, span].astype(jnp.float32)).astype(jnp.bfloat16)
    tcopy.wait()
    turn = table[...]
    width = weight.shape[1] // len(copies)
    for k, copy in enumerate(copies):
        copy.wait()
        both = jnp.dot(
            normed_ref[...], weight[:, width * k : width * (k + 1)], preferred_element_type=jnp.float32
        )
        for part in range(0, width, 2 * HD):
            at = width * k + part
            kv_ref[:, at : at + HD] = turned(both[:, part : part + HD], turn).astype(jnp.bfloat16)
            kv_ref[:, at + HD : at + 2 * HD] = both[:, part + HD : part + 2 * HD].astype(jnp.bfloat16)


def query_kernel(places, normed_ref, table, weight_hbm, next_hbm, query_ref, *refs):
    kept_refs, (weight, wsems, sems) = refs[: len(places)], refs[len(places) :]
    copies = column_copies(weight_hbm, weight, wsems)
    next_copies = output_copies(next_hbm, kept_refs, sems, [peer_place(*p) for p in places])
    for copy in copies + next_copies:
        copy.start()
    turn = table[...]
    width = weight.shape[1] // len(copies)
    for k, copy in enumerate(copies):
        copy.wait()
        both = jnp.dot(
            normed_ref[...], weight[:, width * k : width * (k + 1)], preferred_element_type=jnp.float32
        )
        for part in range(0, width, HD):
            at = width * k + part
            query_ref[:, at : at + HD] = turned(both[:, part : part + HD], turn).astype(jnp.bfloat16)
    for copy in next_copies:
        copy.wait()


def output_copies(weight_hbm, weights, sems, places):
    return [
        pltpu.make_async_copy(
            weight_hbm.at[0, :, pl.ds(pl.multiple_of(place, 128), weight.shape[1])], weight, sems.at[k]
        )
        for k, (weight, place) in enumerate(zip(weights, places))
    ]


def peer_place(steps, half, start):
    count = lax.axis_size("tp")
    return lax.rem(lax.axis_index("tp") + steps, count) * half + start


def steps_of(width):
    return [(at, min(256, width - at)) for at in range(0, width, 256)]


def multiply(attn_ref, weight_ref, out_ref):
    for at, step in steps_of(weight_ref.shape[1]):
        out_ref[:, at : at + step] = jnp.dot(
            attn_ref[...], weight_ref[:, at : at + step], preferred_element_type=jnp.float32
        ).astype(out_ref.dtype)


def attend_kernel(block_count, places, window_ref, query_ref, *refs):
    peers = lax.axis_size("tp") - 1
    kv_refs, weights, refs = refs[:block_count], refs[block_count : block_count + peers], refs[block_count + peers :]
    weight_hbm, attn_ref, refs = refs[0], refs[1], refs[2:]
    send_refs, kept_refs, sems = refs[:peers], refs[peers:-1], refs[-1]
    copies = output_copies(weight_hbm, kept_refs, sems, [peer_place(*p) for p in places])
    for copy in copies:
        copy.start()
    ctx = lax.axis_index("ctx")

    @pl.when(ctx >= 0)
    def _():
        rows = query_ref.shape[0]
        kv_count = kv_refs[0].shape[1] // (2 * HD)
        group = query_ref.shape[1] // HD // kv_count
        twin = ctx + 1 - 2 * lax.rem(ctx, 2)
        row = lax.broadcasted_iota(jnp.int32, (rows, rows), 0)
        column = lax.broadcasted_iota(jnp.int32, (rows, rows), 1)
        masks = []
        for block in [ctx, twin, ctx - 2, twin - 2, twin - 4][:block_count]:
            distance = row - column + (ctx - block) * rows
            masks.append((distance >= 0) & (distance < window_ref[0]) & (block >= 0))
        inside = jnp.concatenate(masks, axis=1)[None]
        for g in range(kv_count):
            queries = jnp.concatenate(
                [query_ref[:, HD * (group * g + h) : HD * (group * g + h + 1)] for h in range(group)], axis=0
            )
            keys = jnp.concatenate([r[:, 2 * HD * g : 2 * HD * g + HD] for r in kv_refs], axis=0)
            values = jnp.concatenate([r[:, 2 * HD * g + HD : 2 * HD * (g + 1)] for r in kv_refs], axis=0)
            scores = lax.dot_general(
                queries, keys, (((1,), (1,)), ((), ())), preferred_element_type=jnp.float32
            ).reshape(group, rows, block_count * rows)
            scores = jnp.where(inside, scores * (HD ** (-0.5) * LOG2E), jnp.float32(-1e30))
            highest = jnp.max(scores, axis=2, keepdims=True)
            expo = jnp.exp2(scores - highest).astype(jnp.bfloat16).reshape(group * rows, block_count * rows)
            sums = jnp.dot(
                expo, jnp.concatenate([values, jnp.ones_like(values)], axis=1), preferred_element_type=jnp.float32
            )
            out = (sums[:, :HD] * (1.0 / sums[:, HD:])).astype(jnp.bfloat16)
            for h in range(group):
                at = HD * (group * g + h)
                attn_ref[:, at : at + HD] = out[h * rows : (h + 1) * rows]
        for weight, send_ref in zip(weights, send_refs):
            multiply(attn_ref, weight, send_ref)

    for copy in copies:
        copy.wait()


def multiply_kernel(held, places, attn_ref, *refs):
    held_refs, weight_hbm, refs = refs[:held], refs[held], refs[held + 2 :]
    count = held + len(places)
    out_refs, weights = refs[:count], refs[count : count + len(places)]
    pieces = [
        (k, at, step) for k, weight in enumerate(weights) for at, step in steps_of(weight.shape[1])
    ]
    copies = []
    if places:
        copies = output_copies(
            weight_hbm,
            [weights[k].at[:, pl.ds(at, step)] for k, at, step in pieces],
            refs[-1],
            [peer_place(*places[k]) + at for k, at, _ in pieces],
        )
    for copy in copies:
        copy.start()

    @pl.when(lax.axis_index("ctx") >= 0)
    def _():
        for weight_ref, out_ref in zip(held_refs, out_refs):
            multiply(attn_ref, weight_ref, out_ref)

    for copy, (k, at, step) in zip(copies, pieces):
        copy.wait()
        out_ref = out_refs[held + k]
        out_ref[:, at : at + step] = jnp.dot(
            attn_ref[...], weights[k][:, at : at + step], preferred_element_type=jnp.float32
        ).astype(out_ref.dtype)


def add_kernel(own_ref, *refs):
    total = own_ref[...]
    for peer_ref in refs[: lax.axis_size("tp") - 1]:
        total = total + peer_ref[...].astype(jnp.float32)
    refs[-1][...] = total.astype(jnp.bfloat16)


def call(kernel, name, outs, in_specs, scratch, mib, flops=0, moved=0):
    return pl.pallas_call(
        kernel,
        out_shape=outs,
        in_specs=in_specs,
        out_specs=jax.tree.map(lambda _: VMEM, outs),
        scratch_shapes=scratch,
        compiler_params=pltpu.CompilerParams(vmem_limit_bytes=mib * MIB),
        cost_estimate=pl.CostEstimate(flops=flops, bytes_accessed=moved, transcendentals=0),
        name=name,
    )


def moved_by(value, axis, steps):
    count = lax.axis_size(axis)
    return lax.ppermute(value, axis, [(source, (source + steps) % count) for source in range(count)])


def twins(value):
    count = lax.axis_size("ctx")
    return lax.ppermute(value, "ctx", [(source, source ^ 1) for source in range(count)])


def body(hidden_in, norm_gain, query_weight, keyval_weight, output_weight, windows):
    bf16, f32 = jnp.bfloat16, jnp.float32
    dma = pltpu.SemaphoreType.DMA
    _, rows, features = hidden_in.shape
    query_columns = query_weight.shape[2]
    kv_columns = keyval_weight.shape[2]
    ctx_count = lax.axis_size("ctx")
    tp_count = lax.axis_size("tp")
    assert ctx_count % 2 == 0
    table = jnp.asarray(rotary_tables(rows * ctx_count))
    hidden_in, norm_gain, table, query_weight, keyval_weight, output_weight = (
        pltpu.with_memory_space_constraint(value, pltpu.HBM)
        for value in (hidden_in, norm_gain, table, query_weight, keyval_weight, output_weight)
    )
    own_kv, normed, turns = call(
        keyval_kernel,
        "keyval",
        (
            jax.ShapeDtypeStruct((rows, kv_columns), bf16),
            jax.ShapeDtypeStruct((rows, features), bf16),
            jax.ShapeDtypeStruct((rows, 2 * HD), f32),
        ),
        [HBM, HBM, HBM, HBM],
        [
            pltpu.VMEM((rows, features), bf16),
            pltpu.VMEM((1, features), bf16),
            pltpu.VMEM((features, kv_columns), bf16),
            dma((3,)),
            dma((max(1, kv_columns // 512),)),
        ],
        48,
        2 * rows * features * kv_columns,
        2 * features * kv_columns,
    )(hidden_in, norm_gain, table, keyval_weight)
    behind = moved_by(own_kv, "ctx", 2)
    beside = twins(own_kv)
    out_columns = output_weight.shape[2]
    half = out_columns // tp_count
    peers = tp_count - 1
    cuts = [half * sum(SHARES[:j]) // sum(SHARES) // 128 * 128 for j in range(len(SHARES) + 1)]
    widths = [end - start for start, end in zip(cuts, cuts[1:])]
    sends = [[jax.ShapeDtypeStruct((rows, width), bf16)] * peers for width in widths]
    owns = [jax.ShapeDtypeStruct((rows, width), f32) for width in widths]

    def away(j):
        return [(d, half, cuts[j]) for d in range(1, peers + 1)]

    def here(j):
        return [(0, half, cuts[j])]

    def weights_of(j):
        return jax.ShapeDtypeStruct((query_columns, widths[j]), bf16)

    def products(name, outs, attn, held, places, columns, after):
        return call(
            functools.partial(multiply_kernel, len(held), places),
            name,
            outs,
            [VMEM] * (1 + len(held)) + [HBM, VMEM],
            [pltpu.VMEM((query_columns, width), bf16) for width in columns]
            + ([dma((sum(len(steps_of(width)) for width in columns),))] if places else []),
            40,
        )(attn, *held, output_weight, after)

    queries, *held = call(
        functools.partial(query_kernel, away(0) + here(0)),
        "query",
        [jax.ShapeDtypeStruct((rows, query_columns), bf16)] + [weights_of(0)] * (peers + 1),
        [VMEM, VMEM, HBM, HBM],
        [
            pltpu.VMEM((features, query_columns), bf16),
            dma((max(1, query_columns // 512),)),
            dma((peers + 1,)),
        ],
        44,
        2 * rows * features * query_columns,
        2 * features * query_columns,
    )(normed, turns, query_weight, output_weight)
    behind, queries = lax.optimization_barrier((behind, queries))
    behind_beside = twins(behind)
    kv_list = [own_kv, beside, behind, behind_beside]
    if ctx_count > 4:
        kv_list.append(moved_by(behind_beside, "ctx", 2))
    ahead = away(1)
    kept = [weights_of(1)] * peers
    attn, *made = call(
        functools.partial(attend_kernel, len(kv_list), ahead),
        "attend",
        [jax.ShapeDtypeStruct((rows, query_columns), bf16)] + sends[0] + kept,
        [SMEM] + [VMEM] * (1 + len(kv_list) + peers) + [HBM],
        [dma((len(ahead),))],
        36,
    )(windows, queries, *kv_list, *held[:peers], output_weight)
    sent = [made[:peers]]
    sent.append(products("away1", sends[1], attn, made[peers : 2 * peers], [], [], made[0]))
    own, *last = products(
        "own0", owns[:1] + sends[2], attn, held[peers:], away(2), [widths[2]] * peers, sent[1][0]
    )
    sent.append(last)
    came = [[moved_by(value, "tp", d + 1) for d, value in enumerate(values)] for values in sent]
    pieces, totals = [], []
    for j in range(len(widths)):
        parts = [own] + came[j] + pieces[max(0, j - 2) : max(0, j - 1)] + totals[-1:]
        total = call(add_kernel, "add", sends[j][0], [VMEM] * len(parts), [], 16)(*parts)
        totals.append(total)
        pieces.append(moved_by(total, "segment", 1))
        if j + 1 < len(widths):
            (own,) = products("own", owns[j + 1 : j + 2], attn, [], here(j + 1), widths[j + 1 : j + 2], total)
    return jnp.concatenate(pieces, axis=1)[None]


def solution(mesh):
    in_specs = (
        P("segment", "ctx", None),
        P("segment", None),
        P("segment", None, "tp"),
        P("segment", None, "tp"),
        P("segment", "tp", None),
        P("segment"),
    )
    out_specs = P("segment", "ctx", "tp")
    return jax.shard_map(body, mesh=mesh, in_specs=in_specs, out_specs=out_specs, check_vma=False)
```

```python
import functools

import jax
import jax.numpy as jnp
import numpy as np
from jax import lax
from jax.experimental import pallas as pl
from jax.experimental.pallas import tpu as pltpu
from jax.sharding import PartitionSpec as P

HD = 128
REACH = 3
NORM_EPS = 1e-05
SHARES = (5, 6, 5)
LOG2E = 1.4426950408889634
MIB = 1024 * 1024

HBM = pl.BlockSpec(memory_space=pltpu.HBM)
VMEM = pl.BlockSpec(memory_space=pltpu.VMEM)
SMEM = pl.BlockSpec(memory_space=pltpu.SMEM)


def rotary_tables(tokens):
    half = HD // 2
    inverse = 10000.0 ** (-np.arange(half, dtype=np.float32) / np.float32(half))
    angles = np.arange(tokens, dtype=np.float32)[:, None] * inverse.astype(np.float32)[None, :]
    cosine = np.cos(angles.astype(np.float64)).astype(np.float32)
    sine = np.sin(angles.astype(np.float64)).astype(np.float32)
    return np.concatenate([cosine, cosine, -sine, sine], axis=1)


def turned(head, table):
    return head * table[:, :HD] + pltpu.roll(head, HD // 2, 1) * table[:, HD:]


def table_copy(table_hbm, table, sem):
    rows = table.shape[0]
    first = pl.multiple_of(lax.axis_index("ctx") * rows, 8)
    return pltpu.make_async_copy(table_hbm.at[pl.ds(first, rows)], table, sem)


def column_copies(weight_hbm, weight, sems):
    width = weight.shape[1] // sems.shape[0]
    return [
        pltpu.make_async_copy(
            weight_hbm.at[0, :, pl.ds(k * width, width)],
            weight.at[:, pl.ds(k * width, width)],
            sems.at[k],
        )
        for k in range(sems.shape[0])
    ]


def keyval_kernel(
    hidden_hbm, gain_hbm, table_hbm, weight_hbm, kv_ref, normed_ref, table, hidden, gain, weight, sems, wsems
):
    hidden_copy = pltpu.make_async_copy(hidden_hbm.at[0], hidden, sems.at[0])
    hidden_copy.start()
    gain_copy = pltpu.make_async_copy(gain_hbm, gain, sems.at[2])
    gain_copy.start()
    tcopy = table_copy(table_hbm, table, sems.at[1])
    tcopy.start()
    copies = column_copies(weight_hbm, weight, wsems)
    for copy in copies:
        copy.start(priority=1)
    gain_copy.wait()
    hidden_copy.wait()
    rows, features = hidden.shape
    spans = [slice(at, at + HD) for at in range(0, features, HD)]
    squares = jnp.zeros((rows, HD), jnp.float32)
    for span in spans:
        wide = hidden[:, span].astype(jnp.float32)
        squares = squares + wide * wide
    mean = jnp.sum(squares, axis=1, keepdims=True) * (1.0 / features)
    inverse = jnp.broadcast_to(lax.rsqrt(mean + NORM_EPS), (rows, HD))
    for span in spans:
        wide = hidden[:, span].astype(jnp.float32)
        normed_ref[:, span] = (wide * inverse * gain[:, span].astype(jnp.float32)).astype(jnp.bfloat16)
    tcopy.wait()
    turn = table[...]
    width = weight.shape[1] // len(copies)
    for k, copy in enumerate(copies):
        copy.wait()
        both = jnp.dot(
            normed_ref[...], weight[:, width * k : width * (k + 1)], preferred_element_type=jnp.float32
        )
        for part in range(0, width, 2 * HD):
            at = width * k + part
            kv_ref[:, at : at + HD] = turned(both[:, part : part + HD], turn).astype(jnp.bfloat16)
            kv_ref[:, at + HD : at + 2 * HD] = both[:, part + HD : part + 2 * HD].astype(jnp.bfloat16)


def query_kernel(places, normed_ref, table, weight_hbm, next_hbm, query_ref, *refs):
    kept_refs, (weight, wsems, sems) = refs[: len(places)], refs[len(places) :]
    copies = column_copies(weight_hbm, weight, wsems)
    next_copies = output_copies(next_hbm, kept_refs, sems, [peer_place(*p) for p in places])
    for copy in copies + next_copies:
        copy.start()
    turn = table[...]
    width = weight.shape[1] // len(copies)
    for k, copy in enumerate(copies):
        copy.wait()
        both = jnp.dot(
            normed_ref[...], weight[:, width * k : width * (k + 1)], preferred_element_type=jnp.float32
        )
        for part in range(0, width, HD):
            at = width * k + part
            query_ref[:, at : at + HD] = turned(both[:, part : part + HD], turn).astype(jnp.bfloat16)
    for copy in next_copies:
        copy.wait()


def output_copies(weight_hbm, weights, sems, places):
    return [
        pltpu.make_async_copy(
            weight_hbm.at[0, :, pl.ds(pl.multiple_of(place, 128), weight.shape[1])], weight, sems.at[k]
        )
        for k, (weight, place) in enumerate(zip(weights, places))
    ]


def peer_place(steps, half, start):
    count = lax.axis_size("tp")
    return lax.rem(lax.axis_index("tp") + steps, count) * half + start


def steps_of(width):
    return [(at, min(256, width - at)) for at in range(0, width, 256)]


def multiply(attn_ref, weight_ref, out_ref):
    for at, step in steps_of(weight_ref.shape[1]):
        out_ref[:, at : at + step] = jnp.dot(
            attn_ref[...], weight_ref[:, at : at + step], preferred_element_type=jnp.float32
        ).astype(out_ref.dtype)


def attend_kernel(block_count, places, window_ref, query_ref, *refs):
    peers = lax.axis_size("tp") - 1
    kv_refs, weights, refs = refs[:block_count], refs[block_count : block_count + peers], refs[block_count + peers :]
    weight_hbm, attn_ref, refs = refs[0], refs[1], refs[2:]
    send_refs, kept_refs, sems = refs[:peers], refs[peers:-1], refs[-1]
    copies = output_copies(weight_hbm, kept_refs, sems, [peer_place(*p) for p in places])
    for copy in copies:
        copy.start()
    ctx = lax.axis_index("ctx")

    @pl.when(ctx >= 0)
    def _():
        rows = query_ref.shape[0]
        kv_count = kv_refs[0].shape[1] // (2 * HD)
        group = query_ref.shape[1] // HD // kv_count
        twin = ctx + 1 - 2 * lax.rem(ctx, 2)
        row = lax.broadcasted_iota(jnp.int32, (rows, rows), 0)
        column = lax.broadcasted_iota(jnp.int32, (rows, rows), 1)
        masks = []
        for block in [ctx, twin, ctx - 2, twin - 2, twin - 4][:block_count]:
            distance = row - column + (ctx - block) * rows
            masks.append((distance >= 0) & (distance < window_ref[0]) & (block >= 0))
        inside = jnp.concatenate(masks, axis=1)[None]
        for g in range(kv_count):
            queries = jnp.concatenate(
                [query_ref[:, HD * (group * g + h) : HD * (group * g + h + 1)] for h in range(group)], axis=0
            )
            keys = jnp.concatenate([r[:, 2 * HD * g : 2 * HD * g + HD] for r in kv_refs], axis=0)
            values = jnp.concatenate([r[:, 2 * HD * g + HD : 2 * HD * (g + 1)] for r in kv_refs], axis=0)
            scores = lax.dot_general(
                queries, keys, (((1,), (1,)), ((), ())), preferred_element_type=jnp.float32
            ).reshape(group, rows, block_count * rows)
            scores = jnp.where(inside, scores * (HD ** (-0.5) * LOG2E), jnp.float32(-1e30))
            highest = jnp.max(scores, axis=2, keepdims=True)
            expo = jnp.exp2(scores - highest).astype(jnp.bfloat16).reshape(group * rows, block_count * rows)
            sums = jnp.dot(
                expo, jnp.concatenate([values, jnp.ones_like(values)], axis=1), preferred_element_type=jnp.float32
            )
            out = (sums[:, :HD] * (1.0 / sums[:, HD:])).astype(jnp.bfloat16)
            for h in range(group):
                at = HD * (group * g + h)
                attn_ref[:, at : at + HD] = out[h * rows : (h + 1) * rows]
        for weight, send_ref in zip(weights, send_refs):
            multiply(attn_ref, weight, send_ref)

    for copy in copies:
        copy.wait()


def multiply_kernel(held, places, attn_ref, *refs):
    held_refs, weight_hbm, refs = refs[:held], refs[held], refs[held + 2 :]
    count = held + len(places)
    out_refs, weights = refs[:count], refs[count : count + len(places)]
    pieces = [
        (k, at, step) for k, weight in enumerate(weights) for at, step in steps_of(weight.shape[1])
    ]
    copies = []
    if places:
        copies = output_copies(
            weight_hbm,
            [weights[k].at[:, pl.ds(at, step)] for k, at, step in pieces],
            refs[-1],
            [peer_place(*places[k]) + at for k, at, _ in pieces],
        )
    for copy in copies:
        copy.start()

    @pl.when(lax.axis_index("ctx") >= 0)
    def _():
        for weight_ref, out_ref in zip(held_refs, out_refs):
            multiply(attn_ref, weight_ref, out_ref)

    for copy, (k, at, step) in zip(copies, pieces):
        copy.wait()
        out_ref = out_refs[held + k]
        out_ref[:, at : at + step] = jnp.dot(
            attn_ref[...], weights[k][:, at : at + step], preferred_element_type=jnp.float32
        ).astype(out_ref.dtype)


def add_kernel(own_ref, *refs):
    total = own_ref[...]
    for peer_ref in refs[: lax.axis_size("tp") - 1]:
        total = total + peer_ref[...].astype(jnp.float32)
    refs[-1][...] = total.astype(jnp.bfloat16)


def place_kernel(starts, *refs):
    pieces, out_hbm, sems = refs[: len(starts)], refs[-2], refs[-1]
    copies = [
        pltpu.make_async_copy(piece, out_hbm.at[0, :, pl.ds(start, piece.shape[1])], sems.at[k])
        for k, (piece, start) in enumerate(zip(pieces, starts))
    ]
    for copy in copies:
        copy.start()
    for copy in copies:
        copy.wait()


def placed(pieces, starts, shape, before):
    return pl.pallas_call(
        functools.partial(place_kernel, starts),
        out_shape=shape,
        in_specs=[VMEM] * len(pieces) + [HBM] * len(before),
        out_specs=HBM,
        scratch_shapes=[pltpu.SemaphoreType.DMA((len(pieces),))],
        input_output_aliases={len(pieces): 0} if before else {},
        compiler_params=pltpu.CompilerParams(vmem_limit_bytes=16 * MIB),
        name="place",
    )(*pieces, *before)


def call(kernel, name, outs, in_specs, scratch, mib, flops=0, moved=0):
    return pl.pallas_call(
        kernel,
        out_shape=outs,
        in_specs=in_specs,
        out_specs=jax.tree.map(lambda _: VMEM, outs),
        scratch_shapes=scratch,
        compiler_params=pltpu.CompilerParams(vmem_limit_bytes=mib * MIB),
        cost_estimate=pl.CostEstimate(flops=flops, bytes_accessed=moved, transcendentals=0),
        name=name,
    )


def moved_by(value, axis, steps):
    count = lax.axis_size(axis)
    return lax.ppermute(value, axis, [(source, (source + steps) % count) for source in range(count)])


def twins(value):
    count = lax.axis_size("ctx")
    return lax.ppermute(value, "ctx", [(source, source ^ 1) for source in range(count)])


def body(hidden_in, norm_gain, query_weight, keyval_weight, output_weight, windows):
    bf16, f32 = jnp.bfloat16, jnp.float32
    dma = pltpu.SemaphoreType.DMA
    _, rows, features = hidden_in.shape
    query_columns = query_weight.shape[2]
    kv_columns = keyval_weight.shape[2]
    ctx_count = lax.axis_size("ctx")
    tp_count = lax.axis_size("tp")
    assert ctx_count % 2 == 0
    table = jnp.asarray(rotary_tables(rows * ctx_count))
    hidden_in, norm_gain, table, query_weight, keyval_weight, output_weight = (
        pltpu.with_memory_space_constraint(value, pltpu.HBM)
        for value in (hidden_in, norm_gain, table, query_weight, keyval_weight, output_weight)
    )
    own_kv, normed, turns = call(
        keyval_kernel,
        "keyval",
        (
            jax.ShapeDtypeStruct((rows, kv_columns), bf16),
            jax.ShapeDtypeStruct((rows, features), bf16),
            jax.ShapeDtypeStruct((rows, 2 * HD), f32),
        ),
        [HBM, HBM, HBM, HBM],
        [
            pltpu.VMEM((rows, features), bf16),
            pltpu.VMEM((1, features), bf16),
            pltpu.VMEM((features, kv_columns), bf16),
            dma((3,)),
            dma((max(1, kv_columns // 512),)),
        ],
        48,
        2 * rows * features * kv_columns,
        2 * features * kv_columns,
    )(hidden_in, norm_gain, table, keyval_weight)
    behind = moved_by(own_kv, "ctx", 2)
    beside = twins(own_kv)
    out_columns = output_weight.shape[2]
    half = out_columns // tp_count
    peers = tp_count - 1
    cuts = [half * sum(SHARES[:j]) // sum(SHARES) // 128 * 128 for j in range(len(SHARES) + 1)]
    widths = [end - start for start, end in zip(cuts, cuts[1:])]
    sends = [[jax.ShapeDtypeStruct((rows, width), bf16)] * peers for width in widths]
    owns = [jax.ShapeDtypeStruct((rows, width), f32) for width in widths]

    def away(j):
        return [(d, half, cuts[j]) for d in range(1, peers + 1)]

    def here(j):
        return [(0, half, cuts[j])]

    def weights_of(j):
        return jax.ShapeDtypeStruct((query_columns, widths[j]), bf16)

    def products(name, outs, attn, held, places, columns, after):
        return call(
            functools.partial(multiply_kernel, len(held), places),
            name,
            outs,
            [VMEM] * (1 + len(held)) + [HBM, VMEM],
            [pltpu.VMEM((query_columns, width), bf16) for width in columns]
            + ([dma((sum(len(steps_of(width)) for width in columns),))] if places else []),
            40,
        )(attn, *held, output_weight, after)

    queries, *held = call(
        functools.partial(query_kernel, away(0) + here(0)),
        "query",
        [jax.ShapeDtypeStruct((rows, query_columns), bf16)] + [weights_of(0)] * (peers + 1),
        [VMEM, VMEM, HBM, HBM],
        [
            pltpu.VMEM((features, query_columns), bf16),
            dma((max(1, query_columns // 512),)),
            dma((peers + 1,)),
        ],
        44,
        2 * rows * features * query_columns,
        2 * features * query_columns,
    )(normed, turns, query_weight, output_weight)
    behind, queries = lax.optimization_barrier((behind, queries))
    behind_beside = twins(behind)
    kv_list = [own_kv, beside, behind, behind_beside]
    if ctx_count > 4:
        kv_list.append(moved_by(behind_beside, "ctx", 2))
    ahead = away(1)
    kept = [weights_of(1)] * peers
    attn, *made = call(
        functools.partial(attend_kernel, len(kv_list), ahead),
        "attend",
        [jax.ShapeDtypeStruct((rows, query_columns), bf16)] + sends[0] + kept,
        [SMEM] + [VMEM] * (1 + len(kv_list) + peers) + [HBM],
        [dma((len(ahead),))],
        36,
    )(windows, queries, *kv_list, *held[:peers], output_weight)
    sent = [made[:peers]]
    sent.append(products("away1", sends[1], attn, made[peers : 2 * peers], [], [], made[0]))
    own, *last = products(
        "own0", owns[:1] + sends[2], attn, held[peers:], away(2), [widths[2]] * peers, sent[1][0]
    )
    sent.append(last)
    came = [[moved_by(value, "tp", d + 1) for d, value in enumerate(values)] for values in sent]
    pieces, totals = [], []
    for j in range(len(widths)):
        parts = [own] + came[j] + pieces[max(0, j - 2) : max(0, j - 1)] + totals[-1:]
        total = call(add_kernel, "add", sends[j][0], [VMEM] * len(parts), [], 16)(*parts)
        totals.append(total)
        pieces.append(moved_by(total, "segment", 1))
        if j + 1 < len(widths):
            (own,) = products("own", owns[j + 1 : j + 2], attn, [], here(j + 1), widths[j + 1 : j + 2], total)
    shape = jax.ShapeDtypeStruct((1, rows, half), bf16)
    most = placed(pieces[:-1], cuts[:-2], shape, [])
    return placed(pieces[-1:], cuts[-2:-1], shape, [most])


def solution(mesh):
    in_specs = (
        P("segment", "ctx", None),
        P("segment", None),
        P("segment", None, "tp"),
        P("segment", None, "tp"),
        P("segment", "tp", None),
        P("segment"),
    )
    out_specs = P("segment", "ctx", "tp")
    return jax.shard_map(body, mesh=mesh, in_specs=in_specs, out_specs=out_specs, check_vma=False)
```

```python
import functools

import jax
import jax.numpy as jnp
import numpy as np
from jax import lax
from jax.experimental import pallas as pl
from jax.experimental.pallas import tpu as pltpu
from jax.sharding import PartitionSpec as P

HD = 128
REACH = 3
NORM_EPS = 1e-05
SHARES = (5, 6, 5)
LOG2E = 1.4426950408889634
MIB = 1024 * 1024

HBM = pl.BlockSpec(memory_space=pltpu.HBM)
VMEM = pl.BlockSpec(memory_space=pltpu.VMEM)
SMEM = pl.BlockSpec(memory_space=pltpu.SMEM)


def rotary_tables(tokens):
    half = HD // 2
    inverse = 10000.0 ** (-np.arange(half, dtype=np.float32) / np.float32(half))
    angles = np.arange(tokens, dtype=np.float32)[:, None] * inverse.astype(np.float32)[None, :]
    cosine = np.cos(angles.astype(np.float64)).astype(np.float32)
    sine = np.sin(angles.astype(np.float64)).astype(np.float32)
    return np.concatenate([cosine, cosine, -sine, sine], axis=1)


def turned(head, table):
    return head * table[:, :HD] + pltpu.roll(head, HD // 2, 1) * table[:, HD:]


def table_copy(table_hbm, table, sem):
    rows = table.shape[0]
    first = pl.multiple_of(lax.axis_index("ctx") * rows, 8)
    return pltpu.make_async_copy(table_hbm.at[pl.ds(first, rows)], table, sem)


def column_copies(weight_hbm, weight, sems):
    width = weight.shape[1] // sems.shape[0]
    return [
        pltpu.make_async_copy(
            weight_hbm.at[0, :, pl.ds(k * width, width)],
            weight.at[:, pl.ds(k * width, width)],
            sems.at[k],
        )
        for k in range(sems.shape[0])
    ]


def keyval_kernel(
    hidden_hbm, gain_hbm, table_hbm, weight_hbm, kv_ref, normed_ref, table, hidden, gain, weight, sems, wsems
):
    hidden_copy = pltpu.make_async_copy(hidden_hbm.at[0], hidden, sems.at[0])
    hidden_copy.start()
    gain_copy = pltpu.make_async_copy(gain_hbm, gain, sems.at[2])
    gain_copy.start()
    tcopy = table_copy(table_hbm, table, sems.at[1])
    tcopy.start()
    copies = column_copies(weight_hbm, weight, wsems)
    for copy in copies:
        copy.start(priority=1)
    gain_copy.wait()
    hidden_copy.wait()

    @pl.when(lax.axis_index("ctx") >= 0)
    def _():
        rows, features = hidden.shape
        spans = [slice(at, at + HD) for at in range(0, features, HD)]
        squares = jnp.zeros((rows, HD), jnp.float32)
        for span in spans:
            wide = hidden[:, span].astype(jnp.float32)
            squares = squares + wide * wide
        mean = jnp.sum(squares, axis=1, keepdims=True) * (1.0 / features)
        inverse = jnp.broadcast_to(lax.rsqrt(mean + NORM_EPS), (rows, HD))
        for span in spans:
            wide = hidden[:, span].astype(jnp.float32)
            normed_ref[:, span] = (wide * inverse * gain[:, span].astype(jnp.float32)).astype(jnp.bfloat16)

    tcopy.wait()
    width = weight.shape[1] // len(copies)
    for k, copy in enumerate(copies):
        copy.wait()

        @pl.when(lax.axis_index("ctx") >= 0)
        def _(k=k):
            both = jnp.dot(
                normed_ref[...], weight[:, width * k : width * (k + 1)], preferred_element_type=jnp.float32
            )
            for part in range(0, width, 2 * HD):
                at = width * k + part
                kv_ref[:, at : at + HD] = turned(both[:, part : part + HD], table).astype(jnp.bfloat16)
                kv_ref[:, at + HD : at + 2 * HD] = both[:, part + HD : part + 2 * HD].astype(jnp.bfloat16)


def query_kernel(places, normed_ref, table, weight_hbm, next_hbm, query_ref, *refs):
    kept_refs, (weight, wsems, sems) = refs[: len(places)], refs[len(places) :]
    copies = column_copies(weight_hbm, weight, wsems)
    next_copies = output_copies(next_hbm, kept_refs, sems, [peer_place(*p) for p in places])
    for copy in copies + next_copies:
        copy.start()
    turn = table[...]
    width = weight.shape[1] // len(copies)
    for k, copy in enumerate(copies):
        copy.wait()
        both = jnp.dot(
            normed_ref[...], weight[:, width * k : width * (k + 1)], preferred_element_type=jnp.float32
        )
        for part in range(0, width, HD):
            at = width * k + part
            query_ref[:, at : at + HD] = turned(both[:, part : part + HD], turn).astype(jnp.bfloat16)
    for copy in next_copies:
        copy.wait()


def output_copies(weight_hbm, weights, sems, places):
    return [
        pltpu.make_async_copy(
            weight_hbm.at[0, :, pl.ds(pl.multiple_of(place, 128), weight.shape[1])], weight, sems.at[k]
        )
        for k, (weight, place) in enumerate(zip(weights, places))
    ]


def peer_place(steps, half, start):
    count = lax.axis_size("tp")
    return lax.rem(lax.axis_index("tp") + steps, count) * half + start


def steps_of(width):
    return [(at, min(256, width - at)) for at in range(0, width, 256)]


def multiply(attn_ref, weight_ref, out_ref):
    for at, step in steps_of(weight_ref.shape[1]):
        out_ref[:, at : at + step] = jnp.dot(
            attn_ref[...], weight_ref[:, at : at + step], preferred_element_type=jnp.float32
        ).astype(out_ref.dtype)


def attend_kernel(block_count, places, window_ref, query_ref, *refs):
    peers = lax.axis_size("tp") - 1
    kv_refs, weights, refs = refs[:block_count], refs[block_count : block_count + peers], refs[block_count + peers :]
    weight_hbm, attn_ref, refs = refs[0], refs[1], refs[2:]
    send_refs, kept_refs, sems = refs[:peers], refs[peers:-1], refs[-1]
    copies = output_copies(weight_hbm, kept_refs, sems, [peer_place(*p) for p in places])
    for copy in copies:
        copy.start()
    ctx = lax.axis_index("ctx")

    @pl.when(ctx >= 0)
    def _():
        rows = query_ref.shape[0]
        kv_count = kv_refs[0].shape[1] // (2 * HD)
        group = query_ref.shape[1] // HD // kv_count
        twin = ctx + 1 - 2 * lax.rem(ctx, 2)
        row = lax.broadcasted_iota(jnp.int32, (rows, rows), 0)
        column = lax.broadcasted_iota(jnp.int32, (rows, rows), 1)
        masks = []
        for block in [ctx, twin, ctx - 2, twin - 2, twin - 4][:block_count]:
            distance = row - column + (ctx - block) * rows
            masks.append((distance >= 0) & (distance < window_ref[0]) & (block >= 0))
        inside = jnp.concatenate(masks, axis=1)[None]
        for g in range(kv_count):
            queries = jnp.concatenate(
                [query_ref[:, HD * (group * g + h) : HD * (group * g + h + 1)] for h in range(group)], axis=0
            )
            keys = jnp.concatenate([r[:, 2 * HD * g : 2 * HD * g + HD] for r in kv_refs], axis=0)
            values = jnp.concatenate([r[:, 2 * HD * g + HD : 2 * HD * (g + 1)] for r in kv_refs], axis=0)
            scores = lax.dot_general(
                queries, keys, (((1,), (1,)), ((), ())), preferred_element_type=jnp.float32
            ).reshape(group, rows, block_count * rows)
            scores = jnp.where(inside, scores * (HD ** (-0.5) * LOG2E), jnp.float32(-1e30))
            highest = jnp.max(scores, axis=2, keepdims=True)
            expo = jnp.exp2(scores - highest).astype(jnp.bfloat16).reshape(group * rows, block_count * rows)
            sums = jnp.dot(
                expo, jnp.concatenate([values, jnp.ones_like(values)], axis=1), preferred_element_type=jnp.float32
            )
            out = (sums[:, :HD] * (1.0 / sums[:, HD:])).astype(jnp.bfloat16)
            for h in range(group):
                at = HD * (group * g + h)
                attn_ref[:, at : at + HD] = out[h * rows : (h + 1) * rows]
        for weight, send_ref in zip(weights, send_refs):
            multiply(attn_ref, weight, send_ref)

    for copy in copies:
        copy.wait()


def multiply_kernel(held, places, attn_ref, *refs):
    held_refs, weight_hbm, refs = refs[:held], refs[held], refs[held + 2 :]
    count = held + len(places)
    out_refs, weights = refs[:count], refs[count : count + len(places)]
    pieces = [
        (k, at, step) for k, weight in enumerate(weights) for at, step in steps_of(weight.shape[1])
    ]
    copies = []
    if places:
        copies = output_copies(
            weight_hbm,
            [weights[k].at[:, pl.ds(at, step)] for k, at, step in pieces],
            refs[-1],
            [peer_place(*places[k]) + at for k, at, _ in pieces],
        )
    for copy in copies:
        copy.start()

    @pl.when(lax.axis_index("ctx") >= 0)
    def _():
        for weight_ref, out_ref in zip(held_refs, out_refs):
            multiply(attn_ref, weight_ref, out_ref)

    for copy, (k, at, step) in zip(copies, pieces):
        copy.wait()
        out_ref = out_refs[held + k]

        @pl.when(lax.axis_index("ctx") >= 0)
        def _(k=k, at=at, step=step, out_ref=out_ref):
            out_ref[:, at : at + step] = jnp.dot(
                attn_ref[...], weights[k][:, at : at + step], preferred_element_type=jnp.float32
            ).astype(out_ref.dtype)


def add_kernel(own_ref, *refs):
    total = own_ref[...]
    for peer_ref in refs[: lax.axis_size("tp") - 1]:
        total = total + peer_ref[...].astype(jnp.float32)
    refs[-1][...] = total.astype(jnp.bfloat16)


def place_kernel(starts, *refs):
    pieces, out_hbm, sems = refs[: len(starts)], refs[-2], refs[-1]
    copies = [
        pltpu.make_async_copy(piece, out_hbm.at[0, :, pl.ds(start, piece.shape[1])], sems.at[k])
        for k, (piece, start) in enumerate(zip(pieces, starts))
    ]
    for copy in copies:
        copy.start()
    for copy in copies:
        copy.wait()


def placed(pieces, starts, shape, before):
    return pl.pallas_call(
        functools.partial(place_kernel, starts),
        out_shape=shape,
        in_specs=[VMEM] * len(pieces) + [HBM] * len(before),
        out_specs=HBM,
        scratch_shapes=[pltpu.SemaphoreType.DMA((len(pieces),))],
        input_output_aliases={len(pieces): 0} if before else {},
        compiler_params=pltpu.CompilerParams(vmem_limit_bytes=16 * MIB),
        name="place",
    )(*pieces, *before)


def call(kernel, name, outs, in_specs, scratch, mib, flops=0, moved=0):
    return pl.pallas_call(
        kernel,
        out_shape=outs,
        in_specs=in_specs,
        out_specs=jax.tree.map(lambda _: VMEM, outs),
        scratch_shapes=scratch,
        compiler_params=pltpu.CompilerParams(vmem_limit_bytes=mib * MIB),
        cost_estimate=pl.CostEstimate(flops=flops, bytes_accessed=moved, transcendentals=0),
        name=name,
    )


def moved_by(value, axis, steps):
    count = lax.axis_size(axis)
    return lax.ppermute(value, axis, [(source, (source + steps) % count) for source in range(count)])


def twins(value):
    count = lax.axis_size("ctx")
    return lax.ppermute(value, "ctx", [(source, source ^ 1) for source in range(count)])


def body(hidden_in, norm_gain, query_weight, keyval_weight, output_weight, windows):
    bf16, f32 = jnp.bfloat16, jnp.float32
    dma = pltpu.SemaphoreType.DMA
    _, rows, features = hidden_in.shape
    query_columns = query_weight.shape[2]
    kv_columns = keyval_weight.shape[2]
    ctx_count = lax.axis_size("ctx")
    tp_count = lax.axis_size("tp")
    assert ctx_count % 2 == 0
    table = jnp.asarray(rotary_tables(rows * ctx_count))
    hidden_in, norm_gain, table, query_weight, keyval_weight, output_weight = (
        pltpu.with_memory_space_constraint(value, pltpu.HBM)
        for value in (hidden_in, norm_gain, table, query_weight, keyval_weight, output_weight)
    )
    own_kv, normed, turns = call(
        keyval_kernel,
        "keyval",
        (
            jax.ShapeDtypeStruct((rows, kv_columns), bf16),
            jax.ShapeDtypeStruct((rows, features), bf16),
            jax.ShapeDtypeStruct((rows, 2 * HD), f32),
        ),
        [HBM, HBM, HBM, HBM],
        [
            pltpu.VMEM((rows, features), bf16),
            pltpu.VMEM((1, features), bf16),
            pltpu.VMEM((features, kv_columns), bf16),
            dma((3,)),
            dma((kv_columns // (2 * HD),)),
        ],
        48,
        2 * rows * features * kv_columns,
        2 * features * kv_columns,
    )(hidden_in, norm_gain, table, keyval_weight)
    behind = moved_by(own_kv, "ctx", 2)
    beside = twins(own_kv)
    out_columns = output_weight.shape[2]
    half = out_columns // tp_count
    peers = tp_count - 1
    cuts = [half * sum(SHARES[:j]) // sum(SHARES) // 128 * 128 for j in range(len(SHARES) + 1)]
    widths = [end - start for start, end in zip(cuts, cuts[1:])]
    sends = [[jax.ShapeDtypeStruct((rows, width), bf16)] * peers for width in widths]
    owns = [jax.ShapeDtypeStruct((rows, width), f32) for width in widths]

    def away(j):
        return [(d, half, cuts[j]) for d in range(1, peers + 1)]

    def here(j):
        return [(0, half, cuts[j])]

    def weights_of(j):
        return jax.ShapeDtypeStruct((query_columns, widths[j]), bf16)

    def products(name, outs, attn, held, places, columns, after):
        return call(
            functools.partial(multiply_kernel, len(held), places),
            name,
            outs,
            [VMEM] * (1 + len(held)) + [HBM, VMEM],
            [pltpu.VMEM((query_columns, width), bf16) for width in columns]
            + ([dma((sum(len(steps_of(width)) for width in columns),))] if places else []),
            40,
        )(attn, *held, output_weight, after)

    queries, *held = call(
        functools.partial(query_kernel, away(0) + here(0)),
        "query",
        [jax.ShapeDtypeStruct((rows, query_columns), bf16)] + [weights_of(0)] * (peers + 1),
        [VMEM, VMEM, HBM, HBM],
        [
            pltpu.VMEM((features, query_columns), bf16),
            dma((max(1, query_columns // 512),)),
            dma((peers + 1,)),
        ],
        44,
        2 * rows * features * query_columns,
        2 * features * query_columns,
    )(normed, turns, query_weight, output_weight)
    behind, queries = lax.optimization_barrier((behind, queries))
    behind_beside = twins(behind)
    kv_list = [own_kv, beside, behind, behind_beside]
    if ctx_count > 4:
        kv_list.append(moved_by(behind_beside, "ctx", 2))
    ahead = away(1)
    kept = [weights_of(1)] * peers
    attn, *made = call(
        functools.partial(attend_kernel, len(kv_list), ahead),
        "attend",
        [jax.ShapeDtypeStruct((rows, query_columns), bf16)] + sends[0] + kept,
        [SMEM] + [VMEM] * (1 + len(kv_list) + peers) + [HBM],
        [dma((len(ahead),))],
        36,
    )(windows, queries, *kv_list, *held[:peers], output_weight)
    sent = [made[:peers]]
    sent.append(products("away1", sends[1], attn, made[peers : 2 * peers], [], [], made[0]))
    own, *last = products(
        "own0", owns[:1] + sends[2], attn, held[peers:], away(2), [widths[2]] * peers, sent[1][0]
    )
    sent.append(last)
    came = [[moved_by(value, "tp", d + 1) for d, value in enumerate(values)] for values in sent]
    pieces, totals = [], []
    for j in range(len(widths)):
        parts = [own] + came[j] + pieces[max(0, j - 2) : max(0, j - 1)] + totals[-1:]
        total = call(add_kernel, "add", sends[j][0], [VMEM] * len(parts), [], 16)(*parts)
        totals.append(total)
        pieces.append(moved_by(total, "segment", 1))
        if j + 1 < len(widths):
            (own,) = products("own", owns[j + 1 : j + 2], attn, [], here(j + 1), widths[j + 1 : j + 2], total)
    shape = jax.ShapeDtypeStruct((1, rows, half), bf16)
    most = placed(pieces[:-1], cuts[:-2], shape, [])
    return placed(pieces[-1:], cuts[-2:-1], shape, [most])


def solution(mesh):
    in_specs = (
        P("segment", "ctx", None),
        P("segment", None),
        P("segment", None, "tp"),
        P("segment", None, "tp"),
        P("segment", "tp", None),
        P("segment"),
    )
    out_specs = P("segment", "ctx", "tp")
    return jax.shard_map(body, mesh=mesh, in_specs=in_specs, out_specs=out_specs, check_vma=False)
```

```python
import functools

import jax
import jax.numpy as jnp
import numpy as np
from jax import lax
from jax.experimental import pallas as pl
from jax.experimental.pallas import tpu as pltpu
from jax.sharding import PartitionSpec as P

HD = 128
REACH = 3
NORM_EPS = 1e-05
SHARES = (5, 6, 5)
PARTS = 4
LOG2E = 1.4426950408889634
MIB = 1024 * 1024

HBM = pl.BlockSpec(memory_space=pltpu.HBM)
VMEM = pl.BlockSpec(memory_space=pltpu.VMEM)
SMEM = pl.BlockSpec(memory_space=pltpu.SMEM)


def rotary_tables(tokens):
    half = HD // 2
    inverse = 10000.0 ** (-np.arange(half, dtype=np.float32) / np.float32(half))
    angles = np.arange(tokens, dtype=np.float32)[:, None] * inverse.astype(np.float32)[None, :]
    cosine = np.cos(angles.astype(np.float64)).astype(np.float32)
    sine = np.sin(angles.astype(np.float64)).astype(np.float32)
    return np.concatenate([cosine, cosine, -sine, sine], axis=1)


def turned(head, table):
    return head * table[:, :HD] + pltpu.roll(head, HD // 2, 1) * table[:, HD:]


def table_copy(table_hbm, table, sem):
    rows = table.shape[0]
    first = pl.multiple_of(lax.axis_index("ctx") * rows, 8)
    return pltpu.make_async_copy(table_hbm.at[pl.ds(first, rows)], table, sem)


def column_copies(weight_hbm, weight, sems):
    width = weight.shape[1] // sems.shape[0]
    return [
        pltpu.make_async_copy(
            weight_hbm.at[0, :, pl.ds(k * width, width)],
            weight.at[:, pl.ds(k * width, width)],
            sems.at[k],
        )
        for k in range(sems.shape[0])
    ]


def keyval_kernel(
    hidden_hbm, gain_hbm, table_hbm, weight_hbm, kv_ref, normed_ref, table, hidden, gain, weight, sems, wsems
):
    hidden_copy = pltpu.make_async_copy(hidden_hbm.at[0], hidden, sems.at[0])
    hidden_copy.start()
    gain_copy = pltpu.make_async_copy(gain_hbm, gain, sems.at[2])
    gain_copy.start()
    tcopy = table_copy(table_hbm, table, sems.at[1])
    tcopy.start()
    copies = column_copies(weight_hbm, weight, wsems)
    for copy in copies:
        copy.start(priority=1)
    gain_copy.wait()
    hidden_copy.wait()

    @pl.when(lax.axis_index("ctx") >= 0)
    def _():
        rows, features = hidden.shape
        spans = [slice(at, at + HD) for at in range(0, features, HD)]
        squares = jnp.zeros((rows, HD), jnp.float32)
        for span in spans:
            wide = hidden[:, span].astype(jnp.float32)
            squares = squares + wide * wide
        mean = jnp.sum(squares, axis=1, keepdims=True) * (1.0 / features)
        inverse = jnp.broadcast_to(lax.rsqrt(mean + NORM_EPS), (rows, HD))
        for span in spans:
            wide = hidden[:, span].astype(jnp.float32)
            normed_ref[:, span] = (wide * inverse * gain[:, span].astype(jnp.float32)).astype(jnp.bfloat16)

    tcopy.wait()
    width = weight.shape[1] // len(copies)
    for k, copy in enumerate(copies):
        copy.wait()

        @pl.when(lax.axis_index("ctx") >= 0)
        def _(k=k):
            both = jnp.dot(
                normed_ref[...], weight[:, width * k : width * (k + 1)], preferred_element_type=jnp.float32
            )
            for part in range(0, width, 2 * HD):
                at = width * k + part
                kv_ref[:, at : at + HD] = turned(both[:, part : part + HD], table).astype(jnp.bfloat16)
                kv_ref[:, at + HD : at + 2 * HD] = both[:, part + HD : part + 2 * HD].astype(jnp.bfloat16)


def query_kernel(places, normed_ref, table, weight_hbm, next_hbm, query_ref, *refs):
    kept_refs, (weight, wsems, sems) = refs[: len(places)], refs[len(places) :]
    copies = column_copies(weight_hbm, weight, wsems)
    next_copies = output_copies(next_hbm, kept_refs, sems, [peer_place(*p) for p in places])
    for copy in copies + next_copies:
        copy.start()
    turn = table[...]
    width = weight.shape[1] // len(copies)
    for k, copy in enumerate(copies):
        copy.wait()
        both = jnp.dot(
            normed_ref[...], weight[:, width * k : width * (k + 1)], preferred_element_type=jnp.float32
        )
        for part in range(0, width, HD):
            at = width * k + part
            query_ref[:, at : at + HD] = turned(both[:, part : part + HD], turn).astype(jnp.bfloat16)
    for copy in next_copies:
        copy.wait()


def output_copies(weight_hbm, weights, sems, places):
    return [
        pltpu.make_async_copy(
            weight_hbm.at[0, :, pl.ds(pl.multiple_of(place, 128), weight.shape[1])], weight, sems.at[k]
        )
        for k, (weight, place) in enumerate(zip(weights, places))
    ]


def peer_place(steps, half, start):
    count = lax.axis_size("tp")
    return lax.rem(lax.axis_index("tp") + steps, count) * half + start


def steps_of(width):
    return [(at, min(256, width - at)) for at in range(0, width, 256)]


def multiply(attn_ref, weight_ref, out_ref):
    for at, step in steps_of(weight_ref.shape[1]):
        out_ref[:, at : at + step] = jnp.dot(
            attn_ref[...], weight_ref[:, at : at + step], preferred_element_type=jnp.float32
        ).astype(out_ref.dtype)


def attend_kernel(block_count, places, window_ref, query_ref, *refs):
    peers = lax.axis_size("tp") - 1
    kv_refs, weights, refs = refs[:block_count], refs[block_count : block_count + peers], refs[block_count + peers :]
    weight_hbm, attn_ref, refs = refs[0], refs[1], refs[2:]
    send_refs, kept_refs, sems = refs[:peers], refs[peers:-1], refs[-1]
    copies = output_copies(weight_hbm, kept_refs, sems, [peer_place(*p) for p in places])
    for copy in copies:
        copy.start()
    ctx = lax.axis_index("ctx")

    @pl.when(ctx >= 0)
    def _():
        rows = query_ref.shape[0]
        kv_count = kv_refs[0].shape[1] // (2 * HD)
        group = query_ref.shape[1] // HD // kv_count
        twin = ctx + 1 - 2 * lax.rem(ctx, 2)
        row = lax.broadcasted_iota(jnp.int32, (rows, rows), 0)
        column = lax.broadcasted_iota(jnp.int32, (rows, rows), 1)
        masks = []
        for block in [ctx, twin, ctx - 2, twin - 2, twin - 4][:block_count]:
            distance = row - column + (ctx - block) * rows
            masks.append((distance >= 0) & (distance < window_ref[0]) & (block >= 0))
        inside = jnp.concatenate(masks, axis=1)[None]
        for g in range(kv_count):
            queries = jnp.concatenate(
                [query_ref[:, HD * (group * g + h) : HD * (group * g + h + 1)] for h in range(group)], axis=0
            )
            keys = jnp.concatenate([r[:, 2 * HD * g : 2 * HD * g + HD] for r in kv_refs], axis=0)
            values = jnp.concatenate([r[:, 2 * HD * g + HD : 2 * HD * (g + 1)] for r in kv_refs], axis=0)
            scores = lax.dot_general(
                queries, keys, (((1,), (1,)), ((), ())), preferred_element_type=jnp.float32
            ).reshape(group, rows, block_count * rows)
            scores = jnp.where(inside, scores * (HD ** (-0.5) * LOG2E), jnp.float32(-1e30))
            highest = jnp.max(scores, axis=2, keepdims=True)
            expo = jnp.exp2(scores - highest).astype(jnp.bfloat16).reshape(group * rows, block_count * rows)
            sums = jnp.dot(
                expo, jnp.concatenate([values, jnp.ones_like(values)], axis=1), preferred_element_type=jnp.float32
            )
            out = (sums[:, :HD] * (1.0 / sums[:, HD:])).astype(jnp.bfloat16)
            for h in range(group):
                at = HD * (group * g + h)
                attn_ref[:, at : at + HD] = out[h * rows : (h + 1) * rows]
        for weight, send_ref in zip(weights, send_refs):
            multiply(attn_ref, weight, send_ref)

    for copy in copies:
        copy.wait()


def multiply_kernel(held, places, attn_ref, *refs):
    held_refs, weight_hbm, refs = refs[:held], refs[held], refs[held + 2 :]
    count = held + len(places)
    out_refs, weights = refs[:count], refs[count : count + len(places)]
    pieces = [
        (k, at, step) for k, weight in enumerate(weights) for at, step in steps_of(weight.shape[1])
    ]
    copies = []
    if places:
        copies = output_copies(
            weight_hbm,
            [weights[k].at[:, pl.ds(at, step)] for k, at, step in pieces],
            refs[-1],
            [peer_place(*places[k]) + at for k, at, _ in pieces],
        )
    for copy in copies:
        copy.start()

    @pl.when(lax.axis_index("ctx") >= 0)
    def _():
        for weight_ref, out_ref in zip(held_refs, out_refs):
            multiply(attn_ref, weight_ref, out_ref)

    for copy, (k, at, step) in zip(copies, pieces):
        copy.wait()
        out_ref = out_refs[held + k]

        @pl.when(lax.axis_index("ctx") >= 0)
        def _(k=k, at=at, step=step, out_ref=out_ref):
            out_ref[:, at : at + step] = jnp.dot(
                attn_ref[...], weights[k][:, at : at + step], preferred_element_type=jnp.float32
            ).astype(out_ref.dtype)


def add_kernel(own_ref, *refs):
    total = own_ref[...]
    for peer_ref in refs[: lax.axis_size("tp") - 1]:
        total = total + peer_ref[...].astype(jnp.float32)
    refs[-1][...] = total.astype(jnp.bfloat16)


def place_kernel(starts, *refs):
    pieces, out_hbm, sems = refs[: len(starts)], refs[-2], refs[-1]
    rows = pieces[0].shape[0] // PARTS
    copies = [
        pltpu.make_async_copy(
            piece.at[pl.ds(part * rows, rows)],
            out_hbm.at[0, pl.ds(part * rows, rows), pl.ds(start, piece.shape[1])],
            sems.at[k, part],
        )
        for k, (piece, start) in enumerate(zip(pieces, starts))
        for part in range(PARTS)
    ]
    for copy in copies:
        copy.start()
    for copy in copies:
        copy.wait()


def placed(pieces, starts, shape, before):
    return pl.pallas_call(
        functools.partial(place_kernel, starts),
        out_shape=shape,
        in_specs=[VMEM] * len(pieces) + [HBM] * len(before),
        out_specs=HBM,
        scratch_shapes=[pltpu.SemaphoreType.DMA((len(pieces), PARTS))],
        input_output_aliases={len(pieces): 0} if before else {},
        compiler_params=pltpu.CompilerParams(vmem_limit_bytes=16 * MIB),
        name="place",
    )(*pieces, *before)


def call(kernel, name, outs, in_specs, scratch, mib, flops=0, moved=0):
    return pl.pallas_call(
        kernel,
        out_shape=outs,
        in_specs=in_specs,
        out_specs=jax.tree.map(lambda _: VMEM, outs),
        scratch_shapes=scratch,
        compiler_params=pltpu.CompilerParams(vmem_limit_bytes=mib * MIB),
        cost_estimate=pl.CostEstimate(flops=flops, bytes_accessed=moved, transcendentals=0),
        name=name,
    )


def moved_by(value, axis, steps):
    count = lax.axis_size(axis)
    return lax.ppermute(value, axis, [(source, (source + steps) % count) for source in range(count)])


def twins(value):
    count = lax.axis_size("ctx")
    return lax.ppermute(value, "ctx", [(source, source ^ 1) for source in range(count)])


def body(hidden_in, norm_gain, query_weight, keyval_weight, output_weight, windows):
    bf16, f32 = jnp.bfloat16, jnp.float32
    dma = pltpu.SemaphoreType.DMA
    _, rows, features = hidden_in.shape
    query_columns = query_weight.shape[2]
    kv_columns = keyval_weight.shape[2]
    ctx_count = lax.axis_size("ctx")
    tp_count = lax.axis_size("tp")
    assert ctx_count % 2 == 0
    table = jnp.asarray(rotary_tables(rows * ctx_count))
    hidden_in, norm_gain, table, query_weight, keyval_weight, output_weight = (
        pltpu.with_memory_space_constraint(value, pltpu.HBM)
        for value in (hidden_in, norm_gain, table, query_weight, keyval_weight, output_weight)
    )
    own_kv, normed, turns = call(
        keyval_kernel,
        "keyval",
        (
            jax.ShapeDtypeStruct((rows, kv_columns), bf16),
            jax.ShapeDtypeStruct((rows, features), bf16),
            jax.ShapeDtypeStruct((rows, 2 * HD), f32),
        ),
        [HBM, HBM, HBM, HBM],
        [
            pltpu.VMEM((rows, features), bf16),
            pltpu.VMEM((1, features), bf16),
            pltpu.VMEM((features, kv_columns), bf16),
            dma((3,)),
            dma((kv_columns // (2 * HD),)),
        ],
        48,
        2 * rows * features * kv_columns,
        2 * features * kv_columns,
    )(hidden_in, norm_gain, table, keyval_weight)
    behind = moved_by(own_kv, "ctx", 2)
    beside = twins(own_kv)
    out_columns = output_weight.shape[2]
    half = out_columns // tp_count
    peers = tp_count - 1
    cuts = [half * sum(SHARES[:j]) // sum(SHARES) // 128 * 128 for j in range(len(SHARES) + 1)]
    widths = [end - start for start, end in zip(cuts, cuts[1:])]
    sends = [[jax.ShapeDtypeStruct((rows, width), bf16)] * peers for width in widths]
    owns = [jax.ShapeDtypeStruct((rows, width), f32) for width in widths]

    def away(j):
        return [(d, half, cuts[j]) for d in range(1, peers + 1)]

    def here(j):
        return [(0, half, cuts[j])]

    def weights_of(j):
        return jax.ShapeDtypeStruct((query_columns, widths[j]), bf16)

    def products(name, outs, attn, held, places, columns, after):
        return call(
            functools.partial(multiply_kernel, len(held), places),
            name,
            outs,
            [VMEM] * (1 + len(held)) + [HBM, VMEM],
            [pltpu.VMEM((query_columns, width), bf16) for width in columns]
            + ([dma((sum(len(steps_of(width)) for width in columns),))] if places else []),
            40,
        )(attn, *held, output_weight, after)

    queries, *held = call(
        functools.partial(query_kernel, away(0) + here(0)),
        "query",
        [jax.ShapeDtypeStruct((rows, query_columns), bf16)] + [weights_of(0)] * (peers + 1),
        [VMEM, VMEM, HBM, HBM],
        [
            pltpu.VMEM((features, query_columns), bf16),
            dma((max(1, query_columns // 512),)),
            dma((peers + 1,)),
        ],
        44,
        2 * rows * features * query_columns,
        2 * features * query_columns,
    )(normed, turns, query_weight, output_weight)
    behind, queries = lax.optimization_barrier((behind, queries))
    behind_beside = twins(behind)
    kv_list = [own_kv, beside, behind, behind_beside]
    if ctx_count > 4:
        kv_list.append(moved_by(behind_beside, "ctx", 2))
    ahead = away(1)
    kept = [weights_of(1)] * peers
    attn, *made = call(
        functools.partial(attend_kernel, len(kv_list), ahead),
        "attend",
        [jax.ShapeDtypeStruct((rows, query_columns), bf16)] + sends[0] + kept,
        [SMEM] + [VMEM] * (1 + len(kv_list) + peers) + [HBM],
        [dma((len(ahead),))],
        36,
    )(windows, queries, *kv_list, *held[:peers], output_weight)
    sent = [made[:peers]]
    sent.append(products("away1", sends[1], attn, made[peers : 2 * peers], [], [], made[0]))
    own, *last = products(
        "own0", owns[:1] + sends[2], attn, held[peers:], away(2), [widths[2]] * peers, sent[1][0]
    )
    sent.append(last)
    came = [[moved_by(value, "tp", d + 1) for d, value in enumerate(values)] for values in sent]
    pieces, totals = [], []
    for j in range(len(widths)):
        parts = [own] + came[j] + pieces[max(0, j - 2) : max(0, j - 1)] + totals[-1:]
        total = call(add_kernel, "add", sends[j][0], [VMEM] * len(parts), [], 16)(*parts)
        totals.append(total)
        pieces.append(moved_by(total, "segment", 1))
        if j + 1 < len(widths):
            (own,) = products("own", owns[j + 1 : j + 2], attn, [], here(j + 1), widths[j + 1 : j + 2], total)
    shape = jax.ShapeDtypeStruct((1, rows, half), bf16)
    most = placed(pieces[:-1], cuts[:-2], shape, [])
    return placed(pieces[-1:], cuts[-2:-1], shape, [most])


def solution(mesh):
    in_specs = (
        P("segment", "ctx", None),
        P("segment", None),
        P("segment", None, "tp"),
        P("segment", None, "tp"),
        P("segment", "tp", None),
        P("segment"),
    )
    out_specs = P("segment", "ctx", "tp")
    return jax.shard_map(body, mesh=mesh, in_specs=in_specs, out_specs=out_specs, check_vma=False)
```
